128 devices in a mesh: face: 32 (over x, z_hi, y), sub: 4 (over z_lo, core).
Axes of the slice: x: 4, y: 4, z: 4 (z_hi: 2, z_lo: 2; z = z_hi * 2 + z_lo), core: 2. Of those that a mesh axis runs over, the one named last changes fastest.
Arguments:
- pixel_state: bfloat16 [1048576, 256], P(('face', 'sub')), may hold values from -6 to 6
- norm1_gain: float32 [256], replicated, may hold values from 0.1 to 1.9
- w_qkv: bfloat16 [256, 768], replicated, may hold values from -1 to 1
- w_out: bfloat16 [256, 256], replicated, may hold values from -0.375 to 0.375
- shift_offsets: int32 [16384], P(('face', 'sub')), may hold values from 0 to 63
- seam_table: int32 [16384, 8], P(('face', 'sub')), may hold values from 0 to 4095
Outputs:
- layer_out: bfloat16 [1048576, 256], P(('face', 'sub'))
The draws below stay inside these ranges and needn't reach their ends.
Inputs may be any that keep to these rules, and one draw needn't show every extreme that they name: `shift_offsets`: offset within each window that splits its shifted keys between itself and its partner. `seam_table`: index t of a seam neighbour window among the 4096 windows that share the block's low index s.
All inputs are finite; a program needn't handle non-finite values.
Results may differ from the reference program's by a relative error of at most 0.0051.
Values may be sent and summed in bfloat16 or wider, within the bound.
No kernel may reach another device: no remote copies, remote signals or barrier semaphores. Data moves between devices by JAX's collectives and lax.ppermute only.
A program may use at most 128 MiB of HBM per device.

```python
import math
import jax
import jax.numpy as jnp
from jax import lax

C = 256
HEADS = 8
HEAD_DIM = 32
WIN = 64
SEAM = 8
PIX_DEV = 8192
WIN_DEV = 128
PIX = 1048576
WIN_ALL = 16384
N_FACE = 32
N_SUB = 4


def common_signs(key):
    key = jax.random.fold_in(key, 101)
    base = jnp.where(jnp.arange(C) < C // 2, 1, -1).astype(jnp.int32)
    return jax.random.permutation(key, base).astype(jnp.float32)


def draw_w_qkv(key, part):
    direction = common_signs(key)
    key = jax.random.fold_in(key, 3)
    base = jnp.clip(jax.random.normal(jax.random.fold_in(key, 1), (C, 3 * C), jnp.float32), -4.5, 4.5)
    base = base * (1.0 / math.sqrt(C))
    strength = jax.random.uniform(jax.random.fold_in(key, 2), (HEADS,), jnp.float32, 5.0, 10.0)
    flips = jax.random.bernoulli(jax.random.fold_in(key, 4), 0.5, (HEADS, HEAD_DIM))
    column = (jnp.where(flips, 1.0, -1.0) * jnp.sqrt(strength / HEAD_DIM)[:, None]).reshape(C)
    planted = direction[:, None] * column[None, :] * (1.0 / math.sqrt(C))
    joined = jnp.concatenate([base[:, :C] + planted, base[:, C:2 * C] + planted, base[:, 2 * C:]], axis=1)
    return joined.astype(jnp.bfloat16)


def draw_pixel_state(key, part):
    key = jax.random.fold_in(key, 7)
    values = jnp.clip(jax.random.normal(jax.random.fold_in(key, 2), (PIX, C), jnp.float32), -6.0, 6.0)
    return values.astype(jnp.bfloat16)


def set_ends(drawn, own_key, low, high):
    dims = drawn.shape
    index_at = [jax.random.randint(jax.random.fold_in(own_key, axis), (), 0, dims[axis]) for axis in range(len(dims))]
    drawn = drawn.at[tuple(index_at)].set(low)
    longest = dims.index(max(dims))
    index_at[longest] = (index_at[longest] + 1) % dims[longest]
    return drawn.at[tuple(index_at)].set(high)


def bell_draw(own_key, shape, scale, bound, held_as=jnp.bfloat16):
    entries = scale * jax.random.normal(own_key, shape, jnp.float32)
    return jnp.clip(entries, min=-bound, max=bound).astype(held_as)


def setup_inputs(seed: int = 0) -> dict:
    key_of = jax.random.split(jax.random.key(seed), 7)
    pixel_state = draw_pixel_state(jax.random.fold_in(key_of[6], 71), 0)
    norm1_gain = jnp.clip(1.0 + 0.18 * jax.random.normal(key_of[1], (C,), jnp.float32), 0.1, 1.9)
    w_qkv = draw_w_qkv(jax.random.fold_in(key_of[6], 71), 0)
    w_out = bell_draw(key_of[3], (C, C), C ** -0.5, 0.375)
    shift_offsets = set_ends(jax.random.randint(key_of[4], (WIN_ALL,), 0, WIN), jax.random.fold_in(key_of[4], 1), 0, WIN - 1).astype(jnp.int32)
    seam_table = set_ends(jax.random.randint(key_of[5], (WIN_ALL, SEAM), 0, N_FACE * WIN_DEV), jax.random.fold_in(key_of[5], 1), 0, (N_FACE * WIN_DEV) - 1).astype(jnp.int32)
    return {"pixel_state": pixel_state, "norm1_gain": norm1_gain, "w_qkv": w_qkv, "w_out": w_out, "shift_offsets": shift_offsets, "seam_table": seam_table}


def layer_norm(values, gain):
    floats = values.astype(jnp.float32)
    centre = lax.optimization_barrier(jnp.mean(floats, axis=-1, keepdims=True))
    spread = lax.optimization_barrier(jnp.mean((floats - centre) * (floats - centre), axis=-1, keepdims=True))
    return ((floats - centre) * lax.rsqrt(spread + 1e-05) * gain).astype(jnp.bfloat16)

def coarse_pool(keys_values):
    width = keys_values.shape[-1]
    pooled = keys_values.reshape(-1, WIN, width).astype(jnp.float32).sum(axis=1)
    return (pooled / math.sqrt(WIN)).astype(jnp.bfloat16)

def attend(queries, own_kv, partner_kv, offsets, group_kv, seam_kv):
    blocks, width = (queries.shape[0], queries.shape[2])
    head_dim = width // HEADS
    scale = 1.0 / math.sqrt(head_dim)
    query_h = queries.astype(jnp.float32).reshape(blocks, WIN, HEADS, head_dim) * scale
    own_k = own_kv[..., :width].astype(jnp.float32).reshape(blocks, WIN, HEADS, head_dim)
    own_v = own_kv[..., width:].astype(jnp.float32).reshape(blocks, WIN, HEADS, head_dim)
    part_k = partner_kv[..., :width].astype(jnp.float32).reshape(blocks, WIN, HEADS, head_dim)
    part_v = partner_kv[..., width:].astype(jnp.float32).reshape(blocks, WIN, HEADS, head_dim)
    group_k = group_kv[:, :width].astype(jnp.float32).reshape(-1, HEADS, head_dim)
    group_v = group_kv[:, width:].astype(jnp.float32).reshape(-1, HEADS, head_dim)
    seam_k = seam_kv[..., :width].astype(jnp.float32).reshape(blocks, -1, HEADS, head_dim)
    seam_v = seam_kv[..., width:].astype(jnp.float32).reshape(blocks, -1, HEADS, head_dim)
    positions = jnp.arange(WIN, dtype=jnp.int32)
    own_mask = positions[None, :] >= offsets[:, None]
    score_own = jnp.einsum('bqhd,bkhd->bhqk', query_h, own_k)
    score_own = jnp.where(own_mask[:, None, None, :], score_own, -1e+30)
    score_part = jnp.einsum('bqhd,bkhd->bhqk', query_h, part_k)
    score_part = jnp.where(own_mask[:, None, None, :], -1e+30, score_part)
    score_group = jnp.einsum('bqhd,ghd->bhqg', query_h, group_k)
    score_seam = jnp.einsum('bqhd,bshd->bhqs', query_h, seam_k)
    scores = jnp.concatenate([score_own, score_part, score_group, score_seam], axis=-1)
    top = lax.optimization_barrier(jnp.max(scores, axis=-1, keepdims=True))
    weights = jnp.exp(scores - top)
    total = lax.optimization_barrier(jnp.sum(weights, axis=-1))
    rounded = weights.astype(jnp.bfloat16).astype(jnp.float32)
    ngroup = group_k.shape[0]
    mixed = jnp.einsum('bhqk,bkhd->bhqd', rounded[..., :WIN], own_v)
    mixed = mixed + jnp.einsum('bhqk,bkhd->bhqd', rounded[..., WIN:2 * WIN], part_v)
    mixed = mixed + jnp.einsum('bhqg,ghd->bhqd', rounded[..., 2 * WIN:2 * WIN + ngroup], group_v)
    mixed = mixed + jnp.einsum('bhqs,bshd->bhqd', rounded[..., 2 * WIN + ngroup:], seam_v)
    mixed = mixed / total[..., None]
    return jnp.transpose(mixed, (0, 2, 1, 3)).reshape(blocks, WIN, width).astype(jnp.bfloat16)

def finish(state, attended, w_out):
    projected = jnp.dot(attended, w_out, preferred_element_type=jnp.float32)
    return (state.astype(jnp.float32) + projected).astype(jnp.bfloat16)

def reference(pixel_state, norm1_gain, w_qkv, w_out, shift_offsets, seam_table):
    width = C
    by_face = pixel_state.reshape(N_FACE, N_SUB * PIX_DEV, width)

    def project(face_rows):
        normed = layer_norm(face_rows, norm1_gain)
        return jnp.dot(normed, w_qkv[:, width:], preferred_element_type=jnp.float32).astype(jnp.bfloat16)
    kv_all = lax.map(project, by_face)
    coarse_all = coarse_pool(kv_all.reshape(-1, 2 * width)).reshape(N_FACE, N_SUB, WIN_DEV, 2 * width)
    offsets_all = shift_offsets.reshape(N_FACE, N_SUB, WIN_DEV)
    seams_all = seam_table.reshape(N_FACE, N_SUB, WIN_DEV, SEAM)

    def face_step(face_idx):
        state = lax.dynamic_index_in_dim(by_face, face_idx, 0, False)
        normed = layer_norm(state, norm1_gain)
        queries = jnp.dot(normed, w_qkv[:, :width], preferred_element_type=jnp.float32).astype(jnp.bfloat16)
        own_all = lax.dynamic_index_in_dim(kv_all, face_idx, 0, False)
        partner_all = lax.dynamic_index_in_dim(kv_all, jnp.bitwise_xor(face_idx, 1), 0, False)
        group_kv = lax.dynamic_index_in_dim(coarse_all, face_idx, 0, False).reshape(N_SUB * WIN_DEV, 2 * width)
        face_offsets = lax.dynamic_index_in_dim(offsets_all, face_idx, 0, False)
        face_seams = lax.dynamic_index_in_dim(seams_all, face_idx, 0, False)

        def sub_step(sub_idx):
            start = sub_idx * PIX_DEV
            query_rows = lax.dynamic_slice_in_dim(queries, start, PIX_DEV, 0).reshape(WIN_DEV, WIN, width)
            own_rows = lax.dynamic_slice_in_dim(own_all, start, PIX_DEV, 0).reshape(WIN_DEV, WIN, 2 * width)
            part_rows = lax.dynamic_slice_in_dim(partner_all, start, PIX_DEV, 0).reshape(WIN_DEV, WIN, 2 * width)
            offsets = lax.dynamic_index_in_dim(face_offsets, sub_idx, 0, False)
            seam_rows = lax.dynamic_index_in_dim(face_seams, sub_idx, 0, False)
            pool = lax.dynamic_index_in_dim(coarse_all, sub_idx, 1, False).reshape(N_FACE * WIN_DEV, 2 * width)
            seam_kv = jnp.take(pool, seam_rows, axis=0)
            return attend(query_rows, own_rows, part_rows, offsets, group_kv, seam_kv).reshape(PIX_DEV, width)
        attended = lax.map(sub_step, jnp.arange(N_SUB).astype(jnp.int32)).reshape(-1, width)
        return finish(state, attended, w_out)
    layer_out = lax.map(face_step, jnp.arange(N_FACE).astype(jnp.int32))
    return layer_out.reshape(PIX, width)
```

```python
import functools
import math

import jax
import jax.numpy as jnp
from jax import lax
from jax.experimental import pallas as pl
from jax.experimental.pallas import tpu as pltpu
from jax.sharding import PartitionSpec as P

HEADS = 8
HALF = HEADS // 2
DIM = 32
C = 256
WIN = 64
SEAM = 8
EPS = 1e-05
SCALE = math.log2(math.e) / math.sqrt(DIM)
BF = jnp.bfloat16
F32 = jnp.float32
LOW = 2.0 ** -60
HIGH = 2.0 ** 60
NEG = -1e30
MB = 1024 * 1024


def params(limit):
    return pltpu.CompilerParams(vmem_limit_bytes=limit * MB)


def exp2(x):
    return jnp.exp2(x)


def dot(a, b):
    return jnp.dot(a, b, preferred_element_type=F32)


def dot_nt(a, b):
    return lax.dot_general(a, b, (((1,), (1,)), ((), ())), preferred_element_type=F32)


def norm_rows(x, gain):
    centre = jnp.mean(x, axis=-1, keepdims=True)
    x = x - centre
    spread = jnp.mean(x * x, axis=-1, keepdims=True)
    return (x * lax.rsqrt(spread + EPS) * gain).astype(BF)


def first_body(x_ref, gain_ref, wq_ref, q_ref, pooled_ref):
    rows = x_ref.shape[0]
    normed = norm_rows(x_ref[...].astype(F32), gain_ref[...])
    q_ref[...] = (dot(normed, wq_ref[...]) * SCALE).astype(BF)
    count = rows // WIN
    row = lax.broadcasted_iota(jnp.int32, (count, rows), 1) // WIN
    pick = jnp.where(row == lax.broadcasted_iota(jnp.int32, (count, rows), 0), 1.0, 0.0).astype(BF)
    pooled_ref[...] = (dot(pick, normed) * (1.0 / math.sqrt(WIN))).astype(BF)


def first(x, gain, wq, rows=1024):
    pixels = x.shape[0]
    return pl.pallas_call(
        first_body,
        grid=(pixels // rows,),
        in_specs=[
            pl.BlockSpec((rows, C), lambda i: (i, 0)),
            pl.BlockSpec((1, C), lambda i: (0, 0)),
            pl.BlockSpec((C, C), lambda i: (0, 0)),
        ],
        out_specs=[
            pl.BlockSpec((rows, C), lambda i: (i, 0)),
            pl.BlockSpec((rows // WIN, C), lambda i: (i, 0)),
        ],
        out_shape=[
            jax.ShapeDtypeStruct((pixels, C), BF),
            jax.ShapeDtypeStruct((pixels // WIN, C), BF),
        ],
        compiler_params=params(48),
        cost_estimate=pl.CostEstimate(flops=2 * pixels * C * C, bytes_accessed=4 * pixels * C, transcendentals=0),
        name="norm_queries_pool",
    )(x, gain, wq)


def group_body(g_ref, wk_ref, wv_ref, kt_ref, vo_ref):
    count = g_ref.shape[0]
    g = g_ref[...]
    kt = lax.dot_general(wk_ref[...], g, (((0,), (1,)), ((), ())), preferred_element_type=F32)
    v = dot(g, wv_ref[...])
    feat = lax.broadcasted_iota(jnp.int32, (128, count), 0) // DIM
    lane = lax.broadcasted_iota(jnp.int32, (count, 128), 1) // DIM
    for h in range(HEADS):
        lo = (h // HALF) * 128
        kt_ref[h] = jnp.where(feat == h % HALF, kt[lo:lo + 128], 0.0).astype(BF)
        mine = lane == h % HALF
        vo_ref[h, :, 0:128] = jnp.where(mine, v[:, lo:lo + 128], 0.0).astype(BF)
        vo_ref[h, :, 128:256] = jnp.where(mine, 1.0, 0.0).astype(BF)


def group(g, wk, wv):
    count = g.shape[0]
    return pl.pallas_call(
        group_body,
        out_shape=[
            jax.ShapeDtypeStruct((HEADS, 128, count), BF),
            jax.ShapeDtypeStruct((HEADS, count, C), BF),
        ],
        compiler_params=params(32),
        name="group_keys_values",
    )(g, wk, wv)


def coarse_body(q_ref, kt_ref, vo_ref, acc_ref):
    for half in range(2):
        q = q_ref[:, half * 128:half * 128 + 128]
        total = None
        for k in range(HALF):
            h = half * HALF + k
            weights = exp2(dot(q, kt_ref[h])).astype(BF)
            part = dot(weights, vo_ref[h])
            total = part if total is None else total + part
        acc_ref[:, half * C:half * C + C] = total


def coarse(q, kt, vo, rows=512):
    pixels = q.shape[0]
    count = kt.shape[2]
    return pl.pallas_call(
        coarse_body,
        grid=(pixels // rows,),
        in_specs=[
            pl.BlockSpec((rows, C), lambda i: (i, 0)),
            pl.BlockSpec((HEADS, 128, count), lambda i: (0, 0, 0)),
            pl.BlockSpec((HEADS, count, C), lambda i: (0, 0, 0)),
        ],
        out_specs=pl.BlockSpec((rows, 2 * C), lambda i: (i, 0)),
        out_shape=jax.ShapeDtypeStruct((pixels, 2 * C), F32),
        compiler_params=params(56),
        cost_estimate=pl.CostEstimate(
            flops=4 * pixels * HEADS * count * C, bytes_accessed=10 * pixels * C, transcendentals=pixels * HEADS * count
        ),
        name="group_attention",
    )(q, kt, vo)


def seam_body(index_ref, pool_ref, out_ref):
    rows = index_ref.shape[0]
    step = 1024
    total = jnp.zeros((rows, C), F32)
    for lo in range(0, pool_ref.shape[0], step):
        at = lax.broadcasted_iota(jnp.int32, (rows, step), 1) + lo
        pick = jnp.where(at == index_ref[...], 1.0, 0.0).astype(BF)
        total = total + dot(pick, pool_ref[lo:lo + step])
    out_ref[...] = total.astype(BF)


def seam(index, pool, rows=256):
    count = index.shape[0]
    return pl.pallas_call(
        seam_body,
        grid=(count // rows,),
        in_specs=[
            pl.BlockSpec((rows, 1), lambda i: (i, 0)),
            pl.BlockSpec(pool.shape, lambda i: (0, 0)),
        ],
        out_specs=pl.BlockSpec((rows, C), lambda i: (i, 0)),
        out_shape=jax.ShapeDtypeStruct((count, C), BF),
        compiler_params=params(48),
        name="seam_rows",
    )(index, pool)


def window_body(
    offset_ref, x_ref, part_ref, q_ref, acc_ref, seam_ref, gain_ref, wk_ref, wv_ref, wo_ref, kt_ref, vo_ref,
    out_ref, kbd, vbd, ksm, vsm, sums,
):
    rows = x_ref.shape[0]
    count = rows // WIN
    step = pl.program_id(0)
    head_of_lane = lax.broadcasted_iota(jnp.int32, (1, 128), 1) // DIM
    position = lax.broadcasted_iota(jnp.int32, (WIN, 1), 0)

    @pl.when(step == 0)
    def _():
        for w in range(count):
            for half in range(2):
                for k in range(HALF):
                    ones = jnp.where(head_of_lane == k, 1.0, 0.0).astype(BF)
                    vbd[w, half, k * WIN:k * WIN + WIN, 128:256] = jnp.broadcast_to(ones, (WIN, 128))
        for half in range(2):
            for k in range(HALF):
                ones = jnp.where(head_of_lane == k, 1.0, 0.0).astype(BF)
                vsm[half, k * 32:k * 32 + 32, 128:256] = jnp.broadcast_to(ones, (32, 128))

    x = x_ref[...].astype(F32)
    other = part_ref[...].astype(F32)
    chosen = []
    for w in range(count):
        offset = offset_ref[step * count + w]
        at = slice(w * WIN, w * WIN + WIN)
        chosen.append(jnp.where(position >= offset, x[at], other[at]))
    normed = norm_rows(jnp.concatenate(chosen, axis=0), gain_ref[...])
    keys = dot(normed, wk_ref[...]).astype(BF)
    values = dot(normed, wv_ref[...]).astype(BF)
    seam_k = dot(seam_ref[...], wk_ref[...]).astype(BF)
    seam_v = dot(seam_ref[...], wv_ref[...]).astype(BF)
    zero = jnp.zeros((), BF)
    for half in range(2):
        lo = half * 128
        for k in range(HALF):
            mine = head_of_lane == k
            at = slice(k * 32, k * 32 + 32)
            ksm[half, at, :] = jnp.where(mine, seam_k[:, lo:lo + 128], zero)
            vsm[half, at, 0:128] = jnp.where(mine, seam_v[:, lo:lo + 128], zero)
            for w in range(count):
                rows_w = slice(w * WIN, w * WIN + WIN)
                to = slice(k * WIN, k * WIN + WIN)
                kbd[w, half, to, :] = jnp.where(mine, keys[rows_w, lo:lo + 128], zero)
                vbd[w, half, to, 0:128] = jnp.where(mine, values[rows_w, lo:lo + 128], zero)

    own = (lax.broadcasted_iota(jnp.int32, (rows, 128), 1) % 32) // SEAM == lax.broadcasted_iota(
        jnp.int32, (rows, 128), 0
    ) // WIN

    def window_scores(w, half):
        q = q_ref[w * WIN:w * WIN + WIN, half * 128:half * 128 + 128]
        return dot_nt(q, kbd[w, half])

    def seam_scores(half):
        return dot_nt(q_ref[:, half * 128:half * 128 + 128], ksm[half])

    for half in range(2):
        at = slice(half * C, half * C + C)
        seam_w = jnp.where(own, exp2(seam_scores(half)), 0.0).astype(BF)
        base = acc_ref[:, at] + dot(seam_w, vsm[half])
        for w in range(count):
            weights = exp2(window_scores(w, half)).astype(BF)
            rows_w = slice(w * WIN, w * WIN + WIN)
            sums[rows_w, at] = base[rows_w] + dot(weights, vbd[w, half])

    den = jnp.concatenate([sums[:, 128:256], sums[:, 384:512]], axis=1)
    fine = jnp.where((den >= LOW) & (den <= HIGH), 0.0, 1.0)
    bad = jnp.max(fine)

    @pl.when(bad > 0.0)
    def _():
        for half in range(2):
            at = slice(half * C, half * C + C)
            q = q_ref[:, half * 128:half * 128 + 128]
            scores_s = jnp.where(own, seam_scores(half), NEG)
            scores_w = jnp.concatenate([window_scores(w, half) for w in range(count)], axis=0)
            head_s = lax.broadcasted_iota(jnp.int32, (rows, 128), 1) // 32
            head_w = lax.broadcasted_iota(jnp.int32, (rows, C), 1) // WIN
            tops_s = jnp.zeros((rows, 128), F32)
            tops_w = jnp.zeros((rows, C), F32)
            total = jnp.zeros((rows, C), F32)
            for k in range(HALF):
                h = half * HALF + k
                scores_g = dot(q, kt_ref[h])
                top = jnp.max(scores_g, axis=1, keepdims=True)
                top = jnp.maximum(top, jnp.max(jnp.where(head_s == k, scores_s, NEG), axis=1, keepdims=True))
                top = jnp.maximum(top, jnp.max(jnp.where(head_w == k, scores_w, NEG), axis=1, keepdims=True))
                tops_s = jnp.where(head_s == k, top, tops_s)
                tops_w = jnp.where(head_w == k, top, tops_w)
                total = total + dot(exp2(scores_g - top).astype(BF), vo_ref[h])
            total = total + dot(jnp.where(own, exp2(scores_s - tops_s), 0.0).astype(BF), vsm[half])
            weights = exp2(scores_w - tops_w).astype(BF)
            for w in range(count):
                rows_w = slice(w * WIN, w * WIN + WIN)
                sums[rows_w, at] = total[rows_w] + dot(weights[rows_w], vbd[w, half])

    attended = jnp.concatenate(
        [sums[:, 0:128] / sums[:, 128:256], sums[:, 256:384] / sums[:, 384:512]], axis=1
    ).astype(BF)
    out_ref[...] = (x + dot(attended, wo_ref[...])).astype(BF)


def window(offsets, x, part, q, acc, seam_rows, gain, wk, wv, wo, kt, vo, rows=256):
    pixels = x.shape[0]
    count = rows // WIN
    row = lambda i, s: (i, 0)
    fixed = lambda i, s: (0, 0)
    fixed3 = lambda i, s: (0, 0, 0)
    return pl.pallas_call(
        window_body,
        grid_spec=pltpu.PrefetchScalarGridSpec(
            num_scalar_prefetch=1,
            grid=(pixels // rows,),
            in_specs=[
                pl.BlockSpec((rows, C), row),
                pl.BlockSpec((rows, C), row),
                pl.BlockSpec((rows, C), row),
                pl.BlockSpec((rows, 2 * C), row),
                pl.BlockSpec((count * SEAM, C), row),
                pl.BlockSpec((1, C), fixed),
                pl.BlockSpec((C, C), fixed),
                pl.BlockSpec((C, C), fixed),
                pl.BlockSpec((C, C), fixed),
                pl.BlockSpec(kt.shape, fixed3),
                pl.BlockSpec(vo.shape, fixed3),
            ],
            out_specs=pl.BlockSpec((rows, C), row),
            scratch_shapes=[
                pltpu.VMEM((count, 2, HALF * WIN, 128), BF),
                pltpu.VMEM((count, 2, HALF * WIN, C), BF),
                pltpu.VMEM((2, HALF * 32, 128), BF),
                pltpu.VMEM((2, HALF * 32, C), BF),
                pltpu.VMEM((rows, 2 * C), F32),
            ],
        ),
        out_shape=jax.ShapeDtypeStruct((pixels, C), BF),
        compiler_params=params(56),
        cost_estimate=pl.CostEstimate(flops=40 * pixels * C * C, bytes_accessed=20 * pixels * C, transcendentals=0),
        name="window_attention",
    )(offsets, x, part, q, acc, seam_rows, gain, wk, wv, wo, kt, vo)


def rotation(dx, dz, dy):
    pairs = []
    for f in range(32):
        x, z, y = f // 8, f // 4 % 2, f % 4
        pairs.append((f, (x + dx) % 4 * 8 + (z + dz) % 2 * 4 + (y + dy) % 4))
    return pairs


def gather_face(block):
    for steps in ([(0, 0, 1), (0, 0, 2), (0, 0, 3)], [(0, 1, 0)], [(1, 0, 0), (2, 0, 0), (3, 0, 0)]):
        block = jnp.concatenate([block] + [lax.ppermute(block, "face", rotation(*s)) for s in steps])
    return block


def place_in_pool(index, windows):
    face, local = index // windows, index % windows
    me = lax.axis_index("face")
    dx = (me // 8 - face // 8) % 4
    dz = (me // 4 - face // 4) % 2
    dy = (me - face) % 4
    return ((dx * 2 + dz) * 4 + dy) * windows + local


def local(pixel_state, norm1_gain, w_qkv, w_out, shift_offsets, seam_table):
    gain = norm1_gain.reshape(1, C)
    wq, wk, wv = w_qkv[:, :C], w_qkv[:, C:2 * C], w_qkv[:, 2 * C:]
    q, pooled = first(pixel_state, gain, wq)
    group_rows = lax.all_gather(pooled, "sub", axis=0, tiled=True)
    pool = gather_face(pooled)
    part = lax.ppermute(pixel_state, "face", [(i, i ^ 1) for i in range(32)])
    kt, vo = group(group_rows, wk, wv)
    acc = coarse(q, kt, vo)
    index = place_in_pool(seam_table, pooled.shape[0]).reshape(-1, 1)
    seam_rows = seam(index, pool)
    return window(shift_offsets, pixel_state, part, q, acc, seam_rows, gain, wk, wv, w_out, kt, vo)


def solution(mesh):
    return jax.shard_map(
        local,
        mesh=mesh,
        in_specs=(
            P(("face", "sub"), None),
            P(),
            P(),
            P(),
            P(("face", "sub")),
            P(("face", "sub"), None),
        ),
        out_specs=P(("face", "sub"), None),
        check_vma=False,
    )
```

```python
import functools
import math

import jax
import jax.numpy as jnp
from jax import lax
from jax.experimental import pallas as pl
from jax.experimental.pallas import tpu as pltpu
from jax.sharding import PartitionSpec as P

HEADS = 8
HALF = HEADS // 2
DIM = 32
C = 256
WIN = 64
SEAM = 8
EPS = 1e-05
SCALE = math.log2(math.e) / math.sqrt(DIM)
BF = jnp.bfloat16
F32 = jnp.float32
HIGH = 2.0 ** 100
NEG = -1e30
MB = 1024 * 1024
PARTS = ((0, 6144, 4192), (6144, 2048, 1600))
MARK = 16


def params(limit):
    return pltpu.CompilerParams(vmem_limit_bytes=limit * MB)


def exp2(x):
    return jnp.exp2(x)


def dot(a, b):
    return jnp.dot(a, b, preferred_element_type=F32)


def dot_nt(a, b):
    return lax.dot_general(a, b, (((1,), (1,)), ((), ())), preferred_element_type=F32)


def sent(offset):
    return (offset + 7) // 8 * 8


def norm_rows(x, gain):
    centre = jnp.mean(x, axis=-1, keepdims=True)
    x = x - centre
    spread = jnp.mean(x * x, axis=-1, keepdims=True)
    return (x * lax.rsqrt(spread + EPS) * gain).astype(BF)


def pool_body(x_ref, gain_ref, pooled_ref):
    rows = x_ref.shape[0]
    normed = norm_rows(x_ref[...].astype(F32), gain_ref[...])
    count = rows // WIN
    row = lax.broadcasted_iota(jnp.int32, (count, rows), 1) // WIN
    pick = jnp.where(row == lax.broadcasted_iota(jnp.int32, (count, rows), 0), 1.0, 0.0).astype(BF)
    pooled_ref[...] = (dot(pick, normed) * (1.0 / math.sqrt(WIN))).astype(BF)


def pool_rows(x, gain, rows=1024):
    pixels = x.shape[0]
    return pl.pallas_call(
        pool_body,
        grid=(pixels // rows,),
        in_specs=[
            pl.BlockSpec((rows, C), lambda i: (i, 0)),
            pl.BlockSpec((1, C), lambda i: (0, 0)),
        ],
        out_specs=pl.BlockSpec((rows // WIN, C), lambda i: (i, 0)),
        out_shape=jax.ShapeDtypeStruct((pixels // WIN, C), BF),
        compiler_params=params(48),
        cost_estimate=pl.CostEstimate(flops=2 * pixels * C * C, bytes_accessed=4 * pixels * C, transcendentals=0),
        name="norm_pool",
    )(x, gain)


def pack_body(first, offset_ref, x_ref, main_ref, rest_ref, packed, at_row):
    step = pl.program_id(0)
    count = x_ref.shape[0] // WIN
    limit = main_ref.shape[0]

    @pl.when(step == 0)
    def _():
        at_row[0] = 0

    start = at_row[0]
    for w in range(count):
        packed[pl.ds(pl.multiple_of(start, 8), WIN), :] = x_ref[w * WIN:w * WIN + WIN, :].astype(F32)
        start = start + sent(offset_ref[first + step * count + w])
    at_row[0] = start

    @pl.when(step == pl.num_programs(0) - 1)
    def _():
        main_ref[...] = packed[0:limit, :].astype(BF)

        @pl.when(start > limit)
        def _():
            rest_ref[...] = packed[limit:, :].astype(BF)


def pack(part, offsets, x, rows=1024):
    first, run, limit = part
    whole = lambda i, s: (0, 0)
    return pl.pallas_call(
        functools.partial(pack_body, first // WIN),
        grid_spec=pltpu.PrefetchScalarGridSpec(
            num_scalar_prefetch=1,
            grid=(run // rows,),
            in_specs=[pl.BlockSpec((rows, C), lambda i, s: (first // rows + i, 0))],
            out_specs=[pl.BlockSpec((limit, C), whole), pl.BlockSpec((run - limit, C), whole)],
            scratch_shapes=[pltpu.VMEM((run, C), F32), pltpu.SMEM((1,), jnp.int32)],
        ),
        out_shape=[
            jax.ShapeDtypeStruct((limit, C), BF),
            jax.ShapeDtypeStruct((run - limit, C), BF),
        ],
        compiler_params=params(32),
        cost_estimate=pl.CostEstimate(flops=0, bytes_accessed=10 * run * C, transcendentals=0),
        name="pack_rows",
    )(offsets, x)


def join_body(*refs):
    lo = 0
    for ref in refs[:-1]:
        refs[-1][lo:lo + ref.shape[0]] = ref[...]
        lo += ref.shape[0]


def join(*blocks):
    rows = sum(b.shape[0] for b in blocks)
    return pl.pallas_call(
        join_body, out_shape=jax.ShapeDtypeStruct((rows, C), BF), compiler_params=params(32), name="join_blocks"
    )(*blocks)


def group_body(*refs):
    wk_ref, wv_ref, kt_ref, vo_ref = refs[-4:]
    g = jnp.concatenate([ref[...] for ref in refs[:-4]], axis=0)
    count = g.shape[0]
    kt = lax.dot_general(wk_ref[...], g, (((0,), (1,)), ((), ())), preferred_element_type=F32)
    v = dot(g, wv_ref[...])
    feat = lax.broadcasted_iota(jnp.int32, (128, count), 0) // DIM
    lane = lax.broadcasted_iota(jnp.int32, (count, 128), 1) // DIM
    for h in range(HEADS):
        lo = (h // HALF) * 128
        kt_ref[h] = jnp.where(feat == h % HALF, kt[lo:lo + 128], 0.0).astype(BF)
        mine = lane == h % HALF
        vo_ref[h // HALF, h % HALF * count:h % HALF * count + count, 0:128] = jnp.where(mine, v[:, lo:lo + 128], 0.0).astype(BF)
        vo_ref[h // HALF, h % HALF * count:h % HALF * count + count, 128:256] = jnp.where(mine, 1.0, 0.0).astype(BF)


def group(blocks, w_qkv):
    count = sum(b.shape[0] for b in blocks)
    return pl.pallas_call(
        group_body,
        grid=(1,),
        in_specs=[pl.BlockSpec(b.shape, lambda i: (0, 0)) for b in blocks]
        + [pl.BlockSpec((C, C), lambda i: (0, 1)), pl.BlockSpec((C, C), lambda i: (0, 2))],
        out_specs=[
            pl.BlockSpec((HEADS, 128, count), lambda i: (0, 0, 0)),
            pl.BlockSpec((2, HALF * count, C), lambda i: (0, 0, 0)),
        ],
        out_shape=[
            jax.ShapeDtypeStruct((HEADS, 128, count), BF),
            jax.ShapeDtypeStruct((2, HALF * count, C), BF),
        ],
        compiler_params=params(32),
        name="group_keys_values",
    )(*blocks, w_qkv, w_qkv)


def coarse_body(x_ref, gain_ref, wq_ref, kt_ref, vo_ref, after_ref, q_ref, acc_ref):
    del after_ref
    normed = norm_rows(x_ref[...].astype(F32), gain_ref[...])
    q = (dot(normed, wq_ref[...]) * SCALE).astype(BF)
    q_ref[...] = q
    weights = []
    for half in range(2):
        heads = range(half * HALF, half * HALF + HALF)
        mine = q[:, half * 128:half * 128 + 128]
        weights.append(jnp.concatenate([exp2(dot(mine, kt_ref[h])).astype(BF) for h in heads], axis=1))
    for half in range(2):
        acc_ref[:, half * C:half * C + C] = dot(weights[half], vo_ref[half])


def coarse(part, x, gain, w_qkv, kt, vo, after, rows=1024):
    first, pixels, _ = part
    steps = pixels // rows
    count = kt.shape[2]
    return pl.pallas_call(
        coarse_body,
        grid=(steps,),
        in_specs=[
            pl.BlockSpec((rows, C), lambda i: (first // rows + i, 0)),
            pl.BlockSpec((1, C), lambda i: (0, 0)),
            pl.BlockSpec((C, C), lambda i: (0, 0)),
            pl.BlockSpec(kt.shape, lambda i: (0, 0, 0)),
            pl.BlockSpec(vo.shape, lambda i: (0, 0, 0)),
            pl.BlockSpec(memory_space=pl.ANY),
        ],
        out_specs=[
            pl.BlockSpec((rows, C), lambda i: (i, 0)),
            pl.BlockSpec((rows, 2 * C), lambda i: (i, 0)),
        ],
        out_shape=[
            jax.ShapeDtypeStruct((pixels, C), BF),
            jax.ShapeDtypeStruct((pixels, 2 * C), F32),
        ],
        compiler_params=params(60),
        cost_estimate=pl.CostEstimate(
            flops=4 * pixels * HEADS * count * C, bytes_accessed=10 * pixels * C, transcendentals=pixels * HEADS * count
        ),
        name="group_attention",
    )(x, gain, w_qkv, kt, vo, after)


def seam_body(index_ref, *refs):
    out_ref, mark_ref = refs[-2:]
    rows = index_ref.shape[0]
    total = jnp.zeros((rows, C), F32)
    lo = 0
    marks = jnp.zeros((MARK, 128), F32)
    for ref in refs[:-2]:
        step = ref.shape[0]
        for at in range(step // 8 - MARK, step, step // 8):
            marks = jnp.maximum(marks, ref[at:at + MARK, 0:128].astype(F32))
        at = lax.broadcasted_iota(jnp.int32, (rows, step), 1) + lo
        pick = jnp.where(at == index_ref[...], 1.0, 0.0).astype(BF)
        total = total + dot(pick, ref[...])
        lo += step
    out_ref[...] = total.astype(BF)
    mark_ref[...] = marks


def seam(index, pools, rows=256):
    count = index.shape[0]
    return pl.pallas_call(
        seam_body,
        grid=(count // rows,),
        in_specs=[pl.BlockSpec((rows, 1), lambda i: (i, 0))]
        + [pl.BlockSpec(pool.shape, lambda i: (0, 0)) for pool in pools],
        out_specs=[pl.BlockSpec((rows, C), lambda i: (i, 0)), pl.BlockSpec((MARK, 128), lambda i: (0, 0))],
        out_shape=[jax.ShapeDtypeStruct((count, C), BF), jax.ShapeDtypeStruct((MARK, 128), F32)],
        compiler_params=params(48),
        name="seam_rows",
    )(index, *pools)


def window_body(
    first, offset_ref, x_ref, main_ref, rest_ref, q_ref, acc_ref, seam_ref, gain_ref, wk_ref, wv_ref, wo_ref,
    kt_hbm, vo_hbm, given_ref, out_ref, kbd, vbd, vsm, ksm, sums, packed, wkt_ref, kt_ref, vo_ref, at_row, done,
):
    del given_ref
    limit = main_ref.shape[0]
    rows = x_ref.shape[0]
    count = rows // WIN
    pairs = count // 2
    near = 2 * SEAM
    step = pl.program_id(0)
    first_window = first + step * count

    def lanes_of(k):
        return jnp.where(lax.broadcasted_iota(jnp.int32, (1, 128), 1) // DIM == k, 1.0, 0.0).astype(BF)

    position = lax.broadcasted_iota(jnp.int32, (WIN, 1), 0)

    @pl.when(step == 0)
    def _():
        at_row[0] = 0
        wkt_ref[...] = wk_ref[...].astype(F32).T.astype(BF)
        packed[0:limit, :] = main_ref[...].astype(F32)

        def add(w, total):
            return total + sent(offset_ref[first + w])

        @pl.when(lax.fori_loop(0, pl.num_programs(0) * count, add, 0) > limit)
        def _():
            packed[limit:, :] = rest_ref[...].astype(F32)

        kbd[...] = jnp.zeros(kbd.shape, BF)
        vsm[...] = jnp.zeros(vsm.shape, BF)
        for half in range(2):
            for k in range(HALF):
                for w in range(count):
                    vbd[w, half, k * WIN:k * WIN + WIN, 128:256] = jnp.broadcast_to(lanes_of(k), (WIN, 128))
                h = half * HALF + k
                for p in range(pairs):
                    vsm[p, h * near:h * near + near, half * C + 128:half * C + C] = jnp.broadcast_to(
                        lanes_of(k), (near, 128)
                    )

    x = x_ref[...].astype(F32)
    chosen = []
    start = at_row[0]
    for w in range(count):
        offset = offset_ref[first_window + w]
        other = packed[pl.ds(pl.multiple_of(start, 8), WIN), :]
        chosen.append(jnp.where(position >= offset, x[w * WIN:w * WIN + WIN], other))
        start = start + sent(offset)
    at_row[0] = start
    normed = norm_rows(jnp.concatenate(chosen, axis=0), gain_ref[...])
    keys = dot_nt(wkt_ref[...], normed)
    values = dot(normed, wv_ref[...]).astype(BF)
    block = (lax.broadcasted_iota(jnp.int32, (64, 128), 0) // DIM) == (
        lax.broadcasted_iota(jnp.int32, (64, 128), 1) // WIN
    )
    first_lanes = lax.broadcasted_iota(jnp.int32, (64, 128), 1) < WIN
    for half in range(2):
        for b in range(2):
            lo = half * 128 + b * 64
            for p in range(pairs):
                pair = keys[lo:lo + 64, p * 128:p * 128 + 128]
                turned = pltpu.roll(pair, WIN, 1)
                to = (half, slice(b * 64, b * 64 + 64), slice(b * 128, b * 128 + 128))
                kbd[(2 * p,) + to] = jnp.where(block, jnp.where(first_lanes, pair, turned), 0.0).astype(BF)
                kbd[(2 * p + 1,) + to] = jnp.where(block, jnp.where(first_lanes, turned, pair), 0.0).astype(BF)
        for k in range(HALF):
            mine = lanes_of(k)
            for w in range(count):
                vbd[w, half, k * WIN:k * WIN + WIN, 0:128] = (
                    values[w * WIN:w * WIN + WIN, half * 128:half * 128 + 128] * mine
                )

    wide = pairs * 128
    seam_k = dot_nt(wkt_ref[...], seam_ref[...]).astype(BF)
    column = lax.broadcasted_iota(jnp.int32, (count * SEAM, wide), 1)
    spread = jnp.where(
        lax.broadcasted_iota(jnp.int32, (count * SEAM, wide), 0) == column // 128 * near + column % near, 1.0, 0.0
    ).astype(BF)
    of_head = (lax.broadcasted_iota(jnp.int32, (C, wide), 1) % 128) // near == (
        lax.broadcasted_iota(jnp.int32, (C, wide), 0) // DIM
    )
    seam_kt = jnp.where(of_head, dot(seam_k, spread), 0.0).astype(BF)
    for p in range(pairs):
        ksm[p] = seam_kt[:, p * 128:p * 128 + 128]
    seam_v = dot(seam_ref[...], wv_ref[...]).astype(BF)
    for h in range(HEADS):
        half, k = h // HALF, h % HALF
        for p in range(pairs):
            vsm[p, h * near:h * near + near, half * C:half * C + 128] = (
                seam_v[p * near:p * near + near, half * 128:half * 128 + 128] * lanes_of(k)
            )
    own = (lax.broadcasted_iota(jnp.int32, (128, 128), 1) % near) // SEAM == (
        lax.broadcasted_iota(jnp.int32, (128, 128), 0) // WIN
    )

    def window_scores(w, half):
        at = pl.ds(pl.multiple_of(w * WIN, WIN), WIN)
        return dot(q_ref[at, half * 128:half * 128 + 128], kbd[w, half])

    def seam_scores(p):
        return dot(q_ref[pl.ds(pl.multiple_of(p * 128, 128), 128), :], ksm[p])

    weights_s = [jnp.where(own, exp2(seam_scores(p)), 0.0).astype(BF) for p in range(pairs)]
    weights_w = [[exp2(window_scores(w, half)).astype(BF) for half in range(2)] for w in range(count)]
    for p in range(pairs):
        sums[p * 128:p * 128 + 128, :] = acc_ref[p * 128:p * 128 + 128, :] + dot(weights_s[p], vsm[p])
    for w in range(count):
        at = slice(w * WIN, w * WIN + WIN)
        for half in range(2):
            sums[at, half * C:half * C + C] += dot(weights_w[w][half], vbd[w, half])

    check = jnp.zeros((8, 128), F32)
    parts = []
    for half in range(2):
        den = sums[:, half * C + 128:half * C + C]
        inverse = 1.0 / den
        check = check + jnp.sum((den + inverse).reshape(rows // 8, 8, 128), axis=0)
        parts.append(sums[:, half * C:half * C + 128] * inverse)
    attended = jnp.concatenate(parts, axis=1).astype(BF)
    out_ref[...] = (x + dot(attended, wo_ref[...])).astype(BF)
    fine = jnp.sum(check) <= HIGH

    @pl.when(jnp.logical_not(fine))
    def _():
        copies = [pltpu.make_async_copy(kt_hbm, kt_ref, done.at[0]), pltpu.make_async_copy(vo_hbm, vo_ref, done.at[1])]
        for copy in copies:
            copy.start()
        for copy in copies:
            copy.wait()
        keys_g = kt_ref.shape[2]
        head_s = lax.broadcasted_iota(jnp.int32, (128, 128), 1) // near
        head_w = lax.broadcasted_iota(jnp.int32, (128, C), 1) // WIN

        def exact(p, carry):
            at = pl.ds(pl.multiple_of(p * 128, 128), 128)
            scores_s = jnp.where(own, seam_scores(p), NEG)
            tops_s = jnp.zeros((128, 128), F32)
            totals = []
            for half in range(2):
                q = q_ref[at, half * 128:half * 128 + 128]
                scores_w = jnp.concatenate([window_scores(2 * p + w, half) for w in range(2)], axis=0)
                tops_w = jnp.zeros((128, C), F32)
                total = jnp.zeros((128, C), F32)
                for k in range(HALF):
                    h = half * HALF + k
                    scores_g = dot(q, kt_ref[h])
                    top = jnp.max(scores_g, axis=1, keepdims=True)
                    top = jnp.maximum(top, jnp.max(jnp.where(head_s == h, scores_s, NEG), axis=1, keepdims=True))
                    top = jnp.maximum(top, jnp.max(jnp.where(head_w == k, scores_w, NEG), axis=1, keepdims=True))
                    tops_s = jnp.where(head_s == h, top, tops_s)
                    tops_w = jnp.where(head_w == k, top, tops_w)
                    total = total + dot(
                        exp2(scores_g - top).astype(BF), vo_ref[half, k * keys_g:k * keys_g + keys_g]
                    )
                weights = exp2(scores_w - tops_w).astype(BF)
                totals.append(total + jnp.concatenate(
                    [dot(weights[w * WIN:w * WIN + WIN], vbd[2 * p + w, half]) for w in range(2)], axis=0
                ))
            weights = jnp.where(own, exp2(jnp.where(own, scores_s - tops_s, NEG)), 0.0).astype(BF)
            total = jnp.concatenate(totals, axis=1) + dot(weights, vsm[p])
            again = jnp.concatenate(
                [total[:, half * C:half * C + 128] / total[:, half * C + 128:half * C + C] for half in range(2)], axis=1
            ).astype(BF)
            out_ref[at, :] = (x_ref[at, :].astype(F32) + dot(again, wo_ref[...])).astype(BF)
            return carry

        lax.fori_loop(0, pairs, exact, 0)


def window(part, offsets, x, main, rest, q, acc, seam_rows, gain, w_qkv, wo, kt, vo, given, rows=1024):
    first, run, _ = part
    pixels = x.shape[0]
    steps = run // rows
    count = rows // WIN
    whole = lambda i, s: (first // rows + i, 0)
    row = lambda i, s: (i, 0)
    fixed = lambda i, s: (0, 0)
    return pl.pallas_call(
        functools.partial(window_body, first // WIN),
        grid_spec=pltpu.PrefetchScalarGridSpec(
            num_scalar_prefetch=1,
            grid=(steps,),
            in_specs=[
                pl.BlockSpec((rows, C), whole),
                pl.BlockSpec(main.shape, fixed),
                pl.BlockSpec(rest.shape, fixed),
                pl.BlockSpec((rows, C), row),
                pl.BlockSpec((rows, 2 * C), row),
                pl.BlockSpec((count * SEAM, C), whole),
                pl.BlockSpec((1, C), fixed),
                pl.BlockSpec((C, C), lambda i, s: (0, 1)),
                pl.BlockSpec((C, C), lambda i, s: (0, 2)),
                pl.BlockSpec((C, C), fixed),
                pl.BlockSpec(memory_space=pl.ANY),
                pl.BlockSpec(memory_space=pl.ANY),
                pl.BlockSpec(memory_space=pl.ANY),
            ],
            out_specs=pl.BlockSpec((rows, C), whole),
            scratch_shapes=[
                pltpu.VMEM((count, 2, 128, C), BF),
                pltpu.VMEM((count, 2, HALF * WIN, C), BF),
                pltpu.VMEM((count // 2, 128, 2 * C), BF),
                pltpu.VMEM((count // 2, C, 128), BF),
                pltpu.VMEM((rows, 2 * C), F32),
                pltpu.VMEM((run, C), F32),
                pltpu.VMEM((C, C), BF),
                pltpu.VMEM(kt.shape, BF),
                pltpu.VMEM(vo.shape, BF),
                pltpu.SMEM((1,), jnp.int32),
                pltpu.SemaphoreType.DMA((2,)),
            ],
        ),
        out_shape=jax.ShapeDtypeStruct((pixels, C), BF),
        input_output_aliases={13: 0} if first else {},
        compiler_params=params(60),
        cost_estimate=pl.CostEstimate(
            flops=40 * run * C * C, bytes_accessed=20 * run * C, transcendentals=0
        ),
        name="window_attention",
    )(offsets, x, main, rest, q, acc, seam_rows, gain, w_qkv, w_qkv, wo, kt, vo, given)


def rotation(dx, dz, dy):
    pairs = []
    for f in range(32):
        x, z, y = f // 8, f // 4 % 2, f % 4
        pairs.append((f, (x + dx) % 4 * 8 + (z + dz) % 2 * 4 + (y + dy) % 4))
    return pairs


def partner(x):
    return lax.ppermute(x, "face", [(i, i ^ 1) for i in range(32)])


def turned(block, steps):
    return [block] + [lax.ppermute(block, "face", rotation(*s)) for s in steps]


def place_in_pool(index, windows):
    face, local = index // windows, index % windows
    me = lax.axis_index("face")
    dx = (me // 8 - face // 8) % 4
    dz = (me // 4 - face // 4) % 2
    dy = (me - face) % 4
    return ((dx * 2 + dz) * 4 + dy) * (windows + MARK) + local


def by_sub(x, k):
    return lax.ppermute(x, "sub", [(i, i ^ k) for i in range(4)])


def local(pixel_state, norm1_gain, w_qkv, w_out, shift_offsets, seam_table):
    gain = norm1_gain.reshape(1, C)
    asked = partner(shift_offsets)
    lengths = sent(shift_offsets)
    over = False
    for first, run, limit in PARTS:
        over = jnp.logical_or(over, lengths[first // WIN:(first + run) // WIN].sum() > limit)
    mark = jnp.broadcast_to(over.astype(BF), (MARK, C))
    mark = functools.reduce(jnp.maximum, [by_sub(mark, k) for k in (1, 2, 3)], mark)
    pooled = pool_rows(pixel_state, gain)
    groups = [pooled] + [by_sub(pooled, k) for k in (1, 2, 3)]
    columns = turned(join(pooled, mark), [(0, 0, 1), (0, 0, 2), (0, 0, 3)])
    mains, rests = zip(*[pack(part, asked, pixel_state) for part in PARTS])
    mains = [partner(main) for main in mains]
    planes = turned(join(*columns), [(0, 1, 0)])
    cube = join(*planes)
    pools = turned(cube, [(1, 0, 0), (2, 0, 0), (3, 0, 0)])
    kt, vo = group(groups, w_qkv)
    late = coarse(PARTS[1], pixel_state, gain, w_qkv, kt, vo, gain)
    early = coarse(PARTS[0], pixel_state, gain, w_qkv, kt, vo, cube)
    index = place_in_pool(seam_table, pooled.shape[0]).reshape(-1, 1)
    seam_rows, marks = seam(index, pools)
    rests = lax.cond(
        marks[0, 0] > 0.0, lambda r: [partner(x) for x in r], lambda r: [jnp.zeros_like(x) for x in r], list(rests)
    )
    out = pixel_state
    for part, main, rest, (q, acc) in zip(PARTS, mains, rests, (early, late)):
        out = window(
            part, shift_offsets, pixel_state, main, rest, q, acc, seam_rows, gain, w_qkv, w_out, kt, vo, out
        )
    return out


def solution(mesh):
    return jax.shard_map(
        local,
        mesh=mesh,
        in_specs=(
            P(("face", "sub"), None),
            P(),
            P(),
            P(),
            P(("face", "sub")),
            P(("face", "sub"), None),
        ),
        out_specs=P(("face", "sub"), None),
        check_vma=False,
    )
```

```python
import functools
import math

import jax
import jax.numpy as jnp
from jax import lax
from jax.experimental import pallas as pl
from jax.experimental.pallas import tpu as pltpu
from jax.sharding import PartitionSpec as P

HEADS = 8
HALF = HEADS // 2
DIM = 32
C = 256
WIN = 64
SEAM = 8
EPS = 1e-05
SCALE = math.log2(math.e) / math.sqrt(DIM)
BF = jnp.bfloat16
F32 = jnp.float32
HIGH = 2.0 ** 100
NEG = -1e30
MB = 1024 * 1024
LIMIT = 5424


def params(limit):
    return pltpu.CompilerParams(vmem_limit_bytes=limit * MB)


def exp2(x):
    return jnp.exp2(x)


def dot(a, b):
    return jnp.dot(a, b, preferred_element_type=F32)


def dot_nt(a, b):
    return lax.dot_general(a, b, (((1,), (1,)), ((), ())), preferred_element_type=F32)


def sent(offset):
    return (offset + 7) // 8 * 8


def norm_rows(x, gain):
    centre = jnp.mean(x, axis=-1, keepdims=True)
    x = x - centre
    spread = jnp.mean(x * x, axis=-1, keepdims=True)
    return (x * lax.rsqrt(spread + EPS) * gain).astype(BF)


def pool_body(x_ref, gain_ref, pooled_ref):
    rows = x_ref.shape[0]
    normed = norm_rows(x_ref[...].astype(F32), gain_ref[...])
    count = rows // WIN
    row = lax.broadcasted_iota(jnp.int32, (count, rows), 1) // WIN
    pick = jnp.where(row == lax.broadcasted_iota(jnp.int32, (count, rows), 0), 1.0, 0.0).astype(BF)
    pooled_ref[...] = (dot(pick, normed) * (1.0 / math.sqrt(WIN))).astype(BF)


def pool_rows(x, gain, rows=2048):
    pixels = x.shape[0]
    return pl.pallas_call(
        pool_body,
        grid=(pixels // rows,),
        in_specs=[
            pl.BlockSpec((rows, C), lambda i: (i, 0)),
            pl.BlockSpec((1, C), lambda i: (0, 0)),
        ],
        out_specs=pl.BlockSpec((rows // WIN, C), lambda i: (i, 0)),
        out_shape=jax.ShapeDtypeStruct((pixels // WIN, C), BF),
        compiler_params=params(60),
        cost_estimate=pl.CostEstimate(flops=2 * pixels * C * C, bytes_accessed=4 * pixels * C, transcendentals=0),
        name="norm_pool",
    )(x, gain)


def pack_body(offset_ref, x_ref, main_ref, rest_ref, packed, at_row):
    step = pl.program_id(0)
    count = x_ref.shape[0] // WIN
    @pl.when(step == 0)
    def _():
        at_row[0] = 0

    start = at_row[0]
    for w in range(count):
        packed[pl.ds(pl.multiple_of(start, 8), WIN), :] = x_ref[w * WIN:w * WIN + WIN, :].astype(F32)
        start = start + sent(offset_ref[step * count + w])
    at_row[0] = start

    @pl.when(step == pl.num_programs(0) - 1)
    def _():
        main_ref[...] = packed[0:LIMIT, :].astype(BF)

        @pl.when(start > LIMIT)
        def _():
            rest_ref[...] = packed[LIMIT:, :].astype(BF)


def pack(offsets, x, rows=4096):
    pixels = x.shape[0]
    whole = lambda i, s: (0, 0)
    return pl.pallas_call(
        pack_body,
        grid_spec=pltpu.PrefetchScalarGridSpec(
            num_scalar_prefetch=1,
            grid=(pixels // rows,),
            in_specs=[pl.BlockSpec((rows, C), lambda i, s: (i, 0))],
            out_specs=[pl.BlockSpec((LIMIT, C), whole), pl.BlockSpec((pixels - LIMIT, C), whole)],
            scratch_shapes=[pltpu.VMEM((pixels, C), F32), pltpu.SMEM((1,), jnp.int32)],
        ),
        out_shape=[
            jax.ShapeDtypeStruct((LIMIT, C), BF),
            jax.ShapeDtypeStruct((pixels - LIMIT, C), BF),
        ],
        compiler_params=params(60),
        cost_estimate=pl.CostEstimate(flops=0, bytes_accessed=10 * pixels * C, transcendentals=0),
        name="pack_rows",
    )(offsets, x)


def join_body(*refs):
    lo = 0
    for ref in refs[:-1]:
        refs[-1][lo:lo + ref.shape[0]] = ref[...]
        lo += ref.shape[0]


def join(*blocks):
    rows = sum(b.shape[0] for b in blocks)
    return pl.pallas_call(
        join_body, out_shape=jax.ShapeDtypeStruct((rows, C), BF), compiler_params=params(32), name="join_blocks"
    )(*blocks)


def group_body(*refs):
    wk_ref, wv_ref, kt_ref, vo_ref = refs[-4:]
    g = jnp.concatenate([ref[...] for ref in refs[:-4]], axis=0)
    count = g.shape[0]
    kt = lax.dot_general(wk_ref[...], g, (((0,), (1,)), ((), ())), preferred_element_type=F32)
    v = dot(g, wv_ref[...])
    feat = lax.broadcasted_iota(jnp.int32, (128, count), 0) // DIM
    lane = lax.broadcasted_iota(jnp.int32, (count, 128), 1) // DIM
    for h in range(HEADS):
        lo = (h // HALF) * 128
        kt_ref[h] = jnp.where(feat == h % HALF, kt[lo:lo + 128], 0.0).astype(BF)
        mine = lane == h % HALF
        vo_ref[h // HALF, h % HALF * count:h % HALF * count + count, 0:128] = jnp.where(mine, v[:, lo:lo + 128], 0.0).astype(BF)
        vo_ref[h // HALF, h % HALF * count:h % HALF * count + count, 128:256] = jnp.where(mine, 1.0, 0.0).astype(BF)


def group(blocks, w_qkv):
    count = sum(b.shape[0] for b in blocks)
    return pl.pallas_call(
        group_body,
        grid=(1,),
        in_specs=[pl.BlockSpec(b.shape, lambda i: (0, 0)) for b in blocks]
        + [pl.BlockSpec((C, C), lambda i: (0, 1)), pl.BlockSpec((C, C), lambda i: (0, 2))],
        out_specs=[
            pl.BlockSpec((HEADS, 128, count), lambda i: (0, 0, 0)),
            pl.BlockSpec((2, HALF * count, C), lambda i: (0, 0, 0)),
        ],
        out_shape=[
            jax.ShapeDtypeStruct((HEADS, 128, count), BF),
            jax.ShapeDtypeStruct((2, HALF * count, C), BF),
        ],
        compiler_params=params(32),
        name="group_keys_values",
    )(*blocks, w_qkv, w_qkv)


def coarse_body(x_ref, next_ref, gain_ref, wq_ref, kt_ref, vo_ref, *refs):
    q_ref, acc_ref, held = refs[-3:]
    step = pl.program_id(0)

    def queries(ref):
        return (dot(norm_rows(ref[...].astype(F32), gain_ref[...]), wq_ref[...]) * SCALE).astype(BF)

    @pl.when(step == 0)
    def _():
        held[...] = queries(x_ref)

    q = held[...]
    q_ref[...] = q
    weights = []
    for half in range(2):
        heads = range(half * HALF, half * HALF + HALF)
        mine = q[:, half * 128:half * 128 + 128]
        weights.append(jnp.concatenate([exp2(dot(mine, kt_ref[h])).astype(BF) for h in heads], axis=1))
    acc_ref[:, 0:C] = dot(weights[0], vo_ref[0])
    acc_ref[:, C:2 * C] = dot(weights[1], vo_ref[1])
    held[...] = queries(next_ref)


def coarse(first, run, x, gain, w_qkv, kt, vo, after, given=(), rows=1024):
    pixels = x.shape[0]
    steps = run // rows
    base = first // rows
    count = kt.shape[2]
    return pl.pallas_call(
        coarse_body,
        grid=(steps,),
        in_specs=[
            pl.BlockSpec((rows, C), lambda i: (base, 0)),
            pl.BlockSpec((rows, C), lambda i: (base + jnp.minimum(i + 1, steps - 1), 0)),
            pl.BlockSpec((1, C), lambda i: (0, 0)),
            pl.BlockSpec((C, C), lambda i: (0, 0)),
            pl.BlockSpec(kt.shape, lambda i: (0, 0, 0)),
            pl.BlockSpec(vo.shape, lambda i: (0, 0, 0)),
        ]
        + [pl.BlockSpec(memory_space=pl.ANY)] * (1 + len(given)),
        out_specs=[
            pl.BlockSpec((rows, C), lambda i: (base + i, 0)),
            pl.BlockSpec((rows, 2 * C), lambda i: (base + i, 0)),
        ],
        out_shape=[
            jax.ShapeDtypeStruct((pixels, C), BF),
            jax.ShapeDtypeStruct((pixels, 2 * C), F32),
        ],
        scratch_shapes=[pltpu.VMEM((rows, C), BF)],
        input_output_aliases={7: 0, 8: 1} if given else {},
        compiler_params=params(60),
        cost_estimate=pl.CostEstimate(
            flops=4 * run * HEADS * count * C, bytes_accessed=10 * run * C, transcendentals=run * HEADS * count
        ),
        name="group_attention",
    )(x, x, gain, w_qkv, kt, vo, after, *given)


def seam_body(index_ref, pool_ref, out_ref):
    rows = index_ref.shape[0]
    step = 1024
    total = jnp.zeros((rows, C), F32)
    for lo in range(0, pool_ref.shape[0], step):
        at = lax.broadcasted_iota(jnp.int32, (rows, step), 1) + lo
        pick = jnp.where(at == index_ref[...], 1.0, 0.0).astype(BF)
        total = total + dot(pick, pool_ref[lo:lo + step])
    out_ref[...] = total.astype(BF)


def seam(index, pool, rows=256):
    count = index.shape[0]
    return pl.pallas_call(
        seam_body,
        grid=(count // rows,),
        in_specs=[
            pl.BlockSpec((rows, 1), lambda i: (i, 0)),
            pl.BlockSpec(pool.shape, lambda i: (0, 0)),
        ],
        out_specs=pl.BlockSpec((rows, C), lambda i: (i, 0)),
        out_shape=jax.ShapeDtypeStruct((count, C), BF),
        compiler_params=params(48),
        name="seam_rows",
    )(index, pool)


def window_body(
    offset_ref, x_ref, main_ref, rest_hbm, q_ref, acc_ref, seam_ref, gain_ref, wk_ref, wv_ref, wo_ref,
    kt_hbm, vo_hbm, out_ref, kbd, vbd, vsm, ksm, sums, packed, rest_ref, wkt_ref, kt_ref, vo_ref, at_row, done,
):
    rows = x_ref.shape[0]
    count = rows // WIN
    pairs = count // 2
    near = 2 * SEAM
    step = pl.program_id(0)
    first_window = step * count

    def lanes_of(k):
        return jnp.where(lax.broadcasted_iota(jnp.int32, (1, 128), 1) // DIM == k, 1.0, 0.0).astype(BF)

    position = lax.broadcasted_iota(jnp.int32, (WIN, 1), 0)

    @pl.when(step == 0)
    def _():
        at_row[0] = 0
        wkt_ref[...] = wk_ref[...].astype(F32).T.astype(BF)
        packed[0:LIMIT, :] = main_ref[...].astype(F32)

        def add(w, total):
            return total + sent(offset_ref[w])

        @pl.when(lax.fori_loop(0, pl.num_programs(0) * count, add, 0) > LIMIT)
        def _():
            copy = pltpu.make_async_copy(rest_hbm, rest_ref, done.at[0])
            copy.start()
            copy.wait()
            packed[LIMIT:, :] = rest_ref[...].astype(F32)

        kbd[...] = jnp.zeros(kbd.shape, BF)
        vsm[...] = jnp.zeros(vsm.shape, BF)
        for half in range(2):
            for k in range(HALF):
                for w in range(count):
                    vbd[w, half, k * WIN:k * WIN + WIN, 128:256] = jnp.broadcast_to(lanes_of(k), (WIN, 128))
                h = half * HALF + k
                for p in range(pairs):
                    vsm[p, h * near:h * near + near, half * C + 128:half * C + C] = jnp.broadcast_to(
                        lanes_of(k), (near, 128)
                    )

    x = x_ref[...].astype(F32)
    chosen = []
    start = at_row[0]
    for w in range(count):
        offset = offset_ref[first_window + w]
        other = packed[pl.ds(pl.multiple_of(start, 8), WIN), :]
        chosen.append(jnp.where(position >= offset, x[w * WIN:w * WIN + WIN], other))
        start = start + sent(offset)
    at_row[0] = start
    normed = norm_rows(jnp.concatenate(chosen, axis=0), gain_ref[...])
    keys = dot_nt(wkt_ref[...], normed)
    values = dot(normed, wv_ref[...]).astype(BF)
    block = (lax.broadcasted_iota(jnp.int32, (64, 128), 0) // DIM) == (
        lax.broadcasted_iota(jnp.int32, (64, 128), 1) // WIN
    )
    first_lanes = lax.broadcasted_iota(jnp.int32, (64, 128), 1) < WIN
    for half in range(2):
        for b in range(2):
            lo = half * 128 + b * 64
            for p in range(pairs):
                pair = keys[lo:lo + 64, p * 128:p * 128 + 128]
                turned = pltpu.roll(pair, WIN, 1)
                to = (half, slice(b * 64, b * 64 + 64), slice(b * 128, b * 128 + 128))
                kbd[(2 * p,) + to] = jnp.where(block, jnp.where(first_lanes, pair, turned), 0.0).astype(BF)
                kbd[(2 * p + 1,) + to] = jnp.where(block, jnp.where(first_lanes, turned, pair), 0.0).astype(BF)
        for k in range(HALF):
            mine = lanes_of(k)
            for w in range(count):
                vbd[w, half, k * WIN:k * WIN + WIN, 0:128] = (
                    values[w * WIN:w * WIN + WIN, half * 128:half * 128 + 128] * mine
                )

    wide = pairs * 128
    seam_k = dot_nt(wkt_ref[...], seam_ref[...]).astype(BF)
    column = lax.broadcasted_iota(jnp.int32, (count * SEAM, wide), 1)
    spread = jnp.where(
        lax.broadcasted_iota(jnp.int32, (count * SEAM, wide), 0) == column // 128 * near + column % near, 1.0, 0.0
    ).astype(BF)
    of_head = (lax.broadcasted_iota(jnp.int32, (C, wide), 1) % 128) // near == (
        lax.broadcasted_iota(jnp.int32, (C, wide), 0) // DIM
    )
    seam_kt = jnp.where(of_head, dot(seam_k, spread), 0.0).astype(BF)
    for p in range(pairs):
        ksm[p] = seam_kt[:, p * 128:p * 128 + 128]
    seam_v = dot(seam_ref[...], wv_ref[...]).astype(BF)
    for h in range(HEADS):
        half, k = h // HALF, h % HALF
        for p in range(pairs):
            vsm[p, h * near:h * near + near, half * C:half * C + 128] = (
                seam_v[p * near:p * near + near, half * 128:half * 128 + 128] * lanes_of(k)
            )
    own = (lax.broadcasted_iota(jnp.int32, (128, 128), 1) % near) // SEAM == (
        lax.broadcasted_iota(jnp.int32, (128, 128), 0) // WIN
    )

    def window_scores(w, half):
        at = pl.ds(pl.multiple_of(w * WIN, WIN), WIN)
        return dot(q_ref[at, half * 128:half * 128 + 128], kbd[w, half])

    def seam_scores(p):
        return dot(q_ref[pl.ds(pl.multiple_of(p * 128, 128), 128), :], ksm[p])

    weights_s = [jnp.where(own, exp2(seam_scores(p)), 0.0).astype(BF) for p in range(pairs)]
    weights_w = [[exp2(window_scores(w, half)).astype(BF) for half in range(2)] for w in range(count)]
    for p in range(pairs):
        sums[p * 128:p * 128 + 128, :] = acc_ref[p * 128:p * 128 + 128, :] + dot(weights_s[p], vsm[p])
    for w in range(count):
        at = slice(w * WIN, w * WIN + WIN)
        for half in range(2):
            sums[at, half * C:half * C + C] += dot(weights_w[w][half], vbd[w, half])

    check = jnp.zeros((8, 128), F32)
    parts = []
    for half in range(2):
        den = sums[:, half * C + 128:half * C + C]
        inverse = 1.0 / den
        check = check + jnp.sum((den + inverse).reshape(rows // 8, 8, 128), axis=0)
        parts.append(sums[:, half * C:half * C + 128] * inverse)
    attended = jnp.concatenate(parts, axis=1).astype(BF)
    out_ref[...] = (x + dot(attended, wo_ref[...])).astype(BF)
    fine = jnp.sum(check) <= HIGH

    @pl.when(jnp.logical_not(fine))
    def _():
        copies = [pltpu.make_async_copy(kt_hbm, kt_ref, done.at[0]), pltpu.make_async_copy(vo_hbm, vo_ref, done.at[1])]
        for copy in copies:
            copy.start()
        for copy in copies:
            copy.wait()
        keys_g = kt_ref.shape[2]
        head_s = lax.broadcasted_iota(jnp.int32, (128, 128), 1) // near
        head_w = lax.broadcasted_iota(jnp.int32, (128, C), 1) // WIN

        def exact(p, carry):
            at = pl.ds(pl.multiple_of(p * 128, 128), 128)
            scores_s = jnp.where(own, seam_scores(p), NEG)
            tops_s = jnp.zeros((128, 128), F32)
            totals = []
            for half in range(2):
                q = q_ref[at, half * 128:half * 128 + 128]
                scores_w = jnp.concatenate([window_scores(2 * p + w, half) for w in range(2)], axis=0)
                tops_w = jnp.zeros((128, C), F32)
                total = jnp.zeros((128, C), F32)
                for k in range(HALF):
                    h = half * HALF + k
                    scores_g = dot(q, kt_ref[h])
                    top = jnp.max(scores_g, axis=1, keepdims=True)
                    top = jnp.maximum(top, jnp.max(jnp.where(head_s == h, scores_s, NEG), axis=1, keepdims=True))
                    top = jnp.maximum(top, jnp.max(jnp.where(head_w == k, scores_w, NEG), axis=1, keepdims=True))
                    tops_s = jnp.where(head_s == h, top, tops_s)
                    tops_w = jnp.where(head_w == k, top, tops_w)
                    total = total + dot(
                        exp2(scores_g - top).astype(BF), vo_ref[half, k * keys_g:k * keys_g + keys_g]
                    )
                weights = exp2(scores_w - tops_w).astype(BF)
                totals.append(total + jnp.concatenate(
                    [dot(weights[w * WIN:w * WIN + WIN], vbd[2 * p + w, half]) for w in range(2)], axis=0
                ))
            weights = jnp.where(own, exp2(jnp.where(own, scores_s - tops_s, NEG)), 0.0).astype(BF)
            total = jnp.concatenate(totals, axis=1) + dot(weights, vsm[p])
            again = jnp.concatenate(
                [total[:, half * C:half * C + 128] / total[:, half * C + 128:half * C + C] for half in range(2)], axis=1
            ).astype(BF)
            out_ref[at, :] = (x_ref[at, :].astype(F32) + dot(again, wo_ref[...])).astype(BF)
            return carry

        lax.fori_loop(0, pairs, exact, 0)


def window(offsets, x, main, rest, q, acc, seam_rows, gain, w_qkv, wo, kt, vo, rows=1024):
    pixels = x.shape[0]
    count = rows // WIN
    row = lambda i, s: (i, 0)
    fixed = lambda i, s: (0, 0)
    return pl.pallas_call(
        window_body,
        grid_spec=pltpu.PrefetchScalarGridSpec(
            num_scalar_prefetch=1,
            grid=(pixels // rows,),
            in_specs=[
                pl.BlockSpec((rows, C), row),
                pl.BlockSpec(main.shape, fixed),
                pl.BlockSpec(memory_space=pl.ANY),
                pl.BlockSpec((rows, C), row),
                pl.BlockSpec((rows, 2 * C), row),
                pl.BlockSpec((count * SEAM, C), row),
                pl.BlockSpec((1, C), fixed),
                pl.BlockSpec((C, C), lambda i, s: (0, 1)),
                pl.BlockSpec((C, C), lambda i, s: (0, 2)),
                pl.BlockSpec((C, C), fixed),
                pl.BlockSpec(memory_space=pl.ANY),
                pl.BlockSpec(memory_space=pl.ANY),
            ],
            out_specs=pl.BlockSpec((rows, C), row),
            scratch_shapes=[
                pltpu.VMEM((count, 2, 128, C), BF),
                pltpu.VMEM((count, 2, HALF * WIN, C), BF),
                pltpu.VMEM((count // 2, 128, 2 * C), BF),
                pltpu.VMEM((count // 2, C, 128), BF),
                pltpu.VMEM((rows, 2 * C), F32),
                pltpu.VMEM((pixels, C), F32),
                pltpu.VMEM(rest.shape, BF),
                pltpu.VMEM((C, C), BF),
                pltpu.VMEM(kt.shape, BF),
                pltpu.VMEM(vo.shape, BF),
                pltpu.SMEM((1,), jnp.int32),
                pltpu.SemaphoreType.DMA((2,)),
            ],
        ),
        out_shape=jax.ShapeDtypeStruct((pixels, C), BF),
        compiler_params=params(60),
        cost_estimate=pl.CostEstimate(
            flops=40 * pixels * C * C, bytes_accessed=20 * pixels * C, transcendentals=0
        ),
        name="window_attention",
    )(offsets, x, main, rest, q, acc, seam_rows, gain, w_qkv, w_qkv, wo, kt, vo)


def rotation(dx, dz, dy):
    pairs = []
    for f in range(32):
        x, z, y = f // 8, f // 4 % 2, f % 4
        pairs.append((f, (x + dx) % 4 * 8 + (z + dz) % 2 * 4 + (y + dy) % 4))
    return pairs


def partner(x):
    return lax.ppermute(x, "face", [(i, i ^ 1) for i in range(32)])


def turned(block, steps):
    return [block] + [lax.ppermute(block, "face", rotation(*s)) for s in steps]


def place_in_pool(index, windows):
    face, local = index // windows, index % windows
    me = lax.axis_index("face")
    dz = (me // 4 - face // 4) % 2
    dy = (me - face) % 4
    return ((face // 8 * 2 + dz) * 4 + dy) * windows + local


def by_sub(x, k):
    return lax.ppermute(x, "sub", [(i, i ^ k) for i in range(4)])


def local(pixel_state, norm1_gain, w_qkv, w_out, shift_offsets, seam_table):
    pixels = pixel_state.shape[0]
    gain = norm1_gain.reshape(1, C)
    asked = partner(shift_offsets)
    more = (jnp.maximum(sent(shift_offsets).sum(), sent(asked).sum()) > LIMIT).astype(jnp.int32)
    pooled = pool_rows(pixel_state, gain)
    groups = [pooled] + [by_sub(pooled, k) for k in (1, 2, 3)]
    columns = turned(pooled, [(0, 0, 1), (0, 0, 2), (0, 0, 3)])
    main, rest = pack(asked, pixel_state)
    main = partner(main)
    planes = turned(join(*columns), [(0, 1, 0)])
    cube = join(*planes)
    lines = [[x * 8 + rest for x in range(4)] for rest in range(8)]
    pool = lax.all_gather(cube, "face", axis=0, tiled=True, axis_index_groups=lines)
    kt, vo = group(groups, w_qkv)
    split = pixels // 4
    sums = coarse(0, split, pixel_state, gain, w_qkv, kt, vo, gain, rows=512)
    q, acc = coarse(split, pixels - split, pixel_state, gain, w_qkv, kt, vo, cube, sums)
    index = place_in_pool(seam_table, pooled.shape[0]).reshape(-1, 1)
    seam_rows = seam(index, pool)
    _, rest = lax.while_loop(lambda c: c[0] > 0, lambda c: (c[0] - 1, partner(c[1])), (more, rest))
    return window(shift_offsets, pixel_state, main, rest, q, acc, seam_rows, gain, w_qkv, w_out, kt, vo)


def solution(mesh):
    return jax.shard_map(
        local,
        mesh=mesh,
        in_specs=(
            P(("face", "sub"), None),
            P(),
            P(),
            P(),
            P(("face", "sub")),
            P(("face", "sub"), None),
        ),
        out_specs=P(("face", "sub"), None),
        check_vma=False,
    )
```

```python
import functools
import math

import jax
import jax.numpy as jnp
from jax import lax
from jax.experimental import pallas as pl
from jax.experimental.pallas import tpu as pltpu
from jax.sharding import PartitionSpec as P

HEADS = 8
HALF = HEADS // 2
DIM = 32
C = 256
WIN = 64
SEAM = 8
EPS = 1e-05
SCALE = math.log2(math.e) / math.sqrt(DIM)
BF = jnp.bfloat16
F32 = jnp.float32
HIGH = 2.0 ** 100
NEG = -1e30
MB = 1024 * 1024
LIMIT = 5424
PIECES = 2


def params(limit):
    return pltpu.CompilerParams(vmem_limit_bytes=limit * MB)


def exp2(x):
    return jnp.exp2(x)


def dot(a, b):
    return jnp.dot(a, b, preferred_element_type=F32)


def dot_nt(a, b):
    return lax.dot_general(a, b, (((1,), (1,)), ((), ())), preferred_element_type=F32)


def sent(offset):
    return (offset + 7) // 8 * 8


def norm_rows(x, gain):
    centre = jnp.mean(x, axis=-1, keepdims=True)
    x = x - centre
    spread = jnp.mean(x * x, axis=-1, keepdims=True)
    return (x * lax.rsqrt(spread + EPS) * gain).astype(BF)


def pool_body(x_ref, gain_ref, pooled_ref):
    rows = x_ref.shape[0]
    normed = norm_rows(x_ref[...].astype(F32), gain_ref[...])
    count = rows // WIN
    row = lax.broadcasted_iota(jnp.int32, (count, rows), 1) // WIN
    pick = jnp.where(row == lax.broadcasted_iota(jnp.int32, (count, rows), 0), 1.0, 0.0).astype(BF)
    pooled_ref[...] = (dot(pick, normed) * (1.0 / math.sqrt(WIN))).astype(BF)


def pool_rows(x, gain, rows=2048):
    pixels = x.shape[0]
    return pl.pallas_call(
        pool_body,
        grid=(pixels // rows,),
        in_specs=[
            pl.BlockSpec((rows, C), lambda i: (i, 0)),
            pl.BlockSpec((1, C), lambda i: (0, 0)),
        ],
        out_specs=pl.BlockSpec((rows // WIN, C), lambda i: (i, 0)),
        out_shape=jax.ShapeDtypeStruct((pixels // WIN, C), BF),
        compiler_params=params(60),
        cost_estimate=pl.CostEstimate(flops=2 * pixels * C * C, bytes_accessed=4 * pixels * C, transcendentals=0),
        name="norm_pool",
    )(x, gain)


def pack_body(offset_ref, mine_ref, x_ref, main_ref, rest_ref, more_ref, packed, at_row):
    step = pl.program_id(0)
    count = x_ref.shape[0] // WIN
    @pl.when(step == 0)
    def _():
        at_row[0] = 0

    start = at_row[0]
    for w in range(count):
        packed[pl.ds(pl.multiple_of(start, 8), WIN), :] = x_ref[w * WIN:w * WIN + WIN, :].astype(F32)
        start = start + sent(offset_ref[step * count + w])
    at_row[0] = start

    @pl.when(step == pl.num_programs(0) - 1)
    def _():
        main_ref[...] = packed[0:LIMIT, :].astype(BF)
        mine = lax.fori_loop(0, mine_ref.shape[0], lambda w, total: total + sent(mine_ref[w]), 0)
        more_ref[0] = (jnp.maximum(start, mine) > LIMIT).astype(jnp.int32)

        @pl.when(start > LIMIT)
        def _():
            rest_ref[...] = packed[LIMIT:, :].astype(BF)


def pack(offsets, mine, x, rows=4096):
    pixels = x.shape[0]
    whole = lambda i, s, t: (0, 0)
    return pl.pallas_call(
        pack_body,
        grid_spec=pltpu.PrefetchScalarGridSpec(
            num_scalar_prefetch=2,
            grid=(pixels // rows,),
            in_specs=[pl.BlockSpec((rows, C), lambda i, s, t: (i, 0))],
            out_specs=[
                pl.BlockSpec((LIMIT, C), whole),
                pl.BlockSpec((pixels - LIMIT, C), whole),
                pl.BlockSpec(memory_space=pltpu.SMEM),
            ],
            scratch_shapes=[pltpu.VMEM((pixels, C), F32), pltpu.SMEM((1,), jnp.int32)],
        ),
        out_shape=[
            jax.ShapeDtypeStruct((LIMIT, C), BF),
            jax.ShapeDtypeStruct((pixels - LIMIT, C), BF),
            jax.ShapeDtypeStruct((1,), jnp.int32),
        ],
        compiler_params=params(60),
        cost_estimate=pl.CostEstimate(flops=0, bytes_accessed=10 * pixels * C, transcendentals=0),
        name="pack_rows",
    )(offsets, mine, x)


def join_body(*refs):
    lo = 0
    for ref in refs[:-1]:
        refs[-1][lo:lo + ref.shape[0]] = ref[...]
        lo += ref.shape[0]


def join(*blocks):
    rows = sum(b.shape[0] for b in blocks)
    return pl.pallas_call(
        join_body, out_shape=jax.ShapeDtypeStruct((rows, C), BF), compiler_params=params(32), name="join_blocks"
    )(*blocks)


def group_body(*refs):
    wk_ref, wv_ref, kt_ref, vo_ref = refs[-4:]
    g = jnp.concatenate([ref[...] for ref in refs[:-4]], axis=0)
    count = g.shape[0]
    kt = lax.dot_general(wk_ref[...], g, (((0,), (1,)), ((), ())), preferred_element_type=F32)
    v = dot(g, wv_ref[...])
    feat = lax.broadcasted_iota(jnp.int32, (128, count), 0) // DIM
    lane = lax.broadcasted_iota(jnp.int32, (count, 128), 1) // DIM
    for h in range(HEADS):
        lo = (h // HALF) * 128
        kt_ref[h] = jnp.where(feat == h % HALF, kt[lo:lo + 128], 0.0).astype(BF)
        mine = lane == h % HALF
        vo_ref[h // HALF, h % HALF * count:h % HALF * count + count, 0:128] = jnp.where(mine, v[:, lo:lo + 128], 0.0).astype(BF)
        vo_ref[h // HALF, h % HALF * count:h % HALF * count + count, 128:256] = jnp.where(mine, 1.0, 0.0).astype(BF)


def group(blocks, w_qkv):
    count = sum(b.shape[0] for b in blocks)
    return pl.pallas_call(
        group_body,
        grid=(1,),
        in_specs=[pl.BlockSpec(b.shape, lambda i: (0, 0)) for b in blocks]
        + [pl.BlockSpec((C, C), lambda i: (0, 1)), pl.BlockSpec((C, C), lambda i: (0, 2))],
        out_specs=[
            pl.BlockSpec((HEADS, 128, count), lambda i: (0, 0, 0)),
            pl.BlockSpec((2, HALF * count, C), lambda i: (0, 0, 0)),
        ],
        out_shape=[
            jax.ShapeDtypeStruct((HEADS, 128, count), BF),
            jax.ShapeDtypeStruct((2, HALF * count, C), BF),
        ],
        compiler_params=params(32),
        name="group_keys_values",
    )(*blocks, w_qkv, w_qkv)


def coarse_body(x_ref, next_ref, gain_ref, wq_ref, kt_ref, vo_ref, *refs):
    q_ref, acc_ref, held = refs[-3:]
    step = pl.program_id(0)

    def queries(ref):
        return (dot(norm_rows(ref[...].astype(F32), gain_ref[...]), wq_ref[...]) * SCALE).astype(BF)

    @pl.when(step == 0)
    def _():
        held[...] = queries(x_ref)

    q = held[...]
    q_ref[...] = q
    weights = []
    for half in range(2):
        heads = range(half * HALF, half * HALF + HALF)
        mine = q[:, half * 128:half * 128 + 128]
        weights.append(jnp.concatenate([exp2(dot(mine, kt_ref[h])).astype(BF) for h in heads], axis=1))
    acc_ref[:, 0:C] = dot(weights[0], vo_ref[0])
    acc_ref[:, C:2 * C] = dot(weights[1], vo_ref[1])
    held[...] = queries(next_ref)


def coarse(first, run, x, gain, w_qkv, kt, vo, after, given=(), rows=1024):
    pixels = x.shape[0]
    steps = run // rows
    base = first // rows
    count = kt.shape[2]
    return pl.pallas_call(
        coarse_body,
        grid=(steps,),
        in_specs=[
            pl.BlockSpec((rows, C), lambda i: (base, 0)),
            pl.BlockSpec((rows, C), lambda i: (base + jnp.minimum(i + 1, steps - 1), 0)),
            pl.BlockSpec((1, C), lambda i: (0, 0)),
            pl.BlockSpec((C, C), lambda i: (0, 0)),
            pl.BlockSpec(kt.shape, lambda i: (0, 0, 0)),
            pl.BlockSpec(vo.shape, lambda i: (0, 0, 0)),
        ]
        + [pl.BlockSpec(memory_space=pl.ANY)] * (1 + len(given)),
        out_specs=[
            pl.BlockSpec((rows, C), lambda i: (base + i, 0)),
            pl.BlockSpec((rows, 2 * C), lambda i: (base + i, 0)),
        ],
        out_shape=[
            jax.ShapeDtypeStruct((pixels, C), BF),
            jax.ShapeDtypeStruct((pixels, 2 * C), F32),
        ],
        scratch_shapes=[pltpu.VMEM((rows, C), BF)],
        input_output_aliases={7: 0, 8: 1} if given else {},
        compiler_params=params(60),
        cost_estimate=pl.CostEstimate(
            flops=4 * run * HEADS * count * C, bytes_accessed=10 * run * C, transcendentals=run * HEADS * count
        ),
        name="group_attention",
    )(x, x, gain, w_qkv, kt, vo, after, *given)


def seam_body(index_ref, *refs):
    out_ref = refs[-1]
    rows = index_ref.shape[0]
    total = jnp.zeros((rows, C), F32)
    lo = 0
    for ref in refs[:-1]:
        step = ref.shape[0]
        at = lax.broadcasted_iota(jnp.int32, (rows, step), 1) + lo
        pick = jnp.where(at == index_ref[...], 1.0, 0.0).astype(BF)
        total = total + dot(pick, ref[...])
        lo += step
    out_ref[...] = total.astype(BF)


def seam(index, pools, rows=256):
    count = index.shape[0]
    return pl.pallas_call(
        seam_body,
        grid=(count // rows,),
        in_specs=[pl.BlockSpec((rows, 1), lambda i: (i, 0))]
        + [pl.BlockSpec(pool.shape, lambda i: (0, 0)) for pool in pools],
        out_specs=pl.BlockSpec((rows, C), lambda i: (i, 0)),
        out_shape=jax.ShapeDtypeStruct((count, C), BF),
        compiler_params=params(48),
        name="seam_rows",
    )(index, *pools)


def window_body(
    offset_ref, x_ref, main_ref, rest_hbm, q_ref, acc_ref, seam_ref, gain_ref, wk_ref, wv_ref, wo_ref,
    kt_hbm, vo_hbm, out_ref, kbd, vbd, vsm, ksm, sums, packed, rest_ref, wkt_ref, kt_ref, vo_ref, at_row, done,
):
    rows = x_ref.shape[0]
    count = rows // WIN
    pairs = count // 2
    near = 2 * SEAM
    step = pl.program_id(0)
    first_window = step * count

    def lanes_of(k):
        return jnp.where(lax.broadcasted_iota(jnp.int32, (1, 128), 1) // DIM == k, 1.0, 0.0).astype(BF)

    position = lax.broadcasted_iota(jnp.int32, (WIN, 1), 0)

    @pl.when(step == 0)
    def _():
        at_row[0] = 0
        wkt_ref[...] = wk_ref[...].astype(F32).T.astype(BF)
        packed[0:LIMIT, :] = main_ref[...].astype(F32)

        def add(w, total):
            return total + sent(offset_ref[w])

        @pl.when(lax.fori_loop(0, pl.num_programs(0) * count, add, 0) > LIMIT)
        def _():
            copy = pltpu.make_async_copy(rest_hbm, rest_ref, done.at[0])
            copy.start()
            copy.wait()
            packed[LIMIT:, :] = rest_ref[...].astype(F32)

        kbd[...] = jnp.zeros(kbd.shape, BF)
        vsm[...] = jnp.zeros(vsm.shape, BF)
        for half in range(2):
            for k in range(HALF):
                for w in range(count):
                    vbd[w, half, k * WIN:k * WIN + WIN, 128:256] = jnp.broadcast_to(lanes_of(k), (WIN, 128))
                h = half * HALF + k
                for p in range(pairs):
                    vsm[p, h * near:h * near + near, half * C + 128:half * C + C] = jnp.broadcast_to(
                        lanes_of(k), (near, 128)
                    )

    block = (lax.broadcasted_iota(jnp.int32, (64, 128), 0) // DIM) == (
        lax.broadcasted_iota(jnp.int32, (64, 128), 1) // WIN
    )
    first_lanes = lax.broadcasted_iota(jnp.int32, (64, 128), 1) < WIN
    own = (lax.broadcasted_iota(jnp.int32, (128, 128), 1) % near) // SEAM == (
        lax.broadcasted_iota(jnp.int32, (128, 128), 0) // WIN
    )
    some = count // PIECES
    some_pairs = some // 2

    def build(piece):
        w0 = piece * some
        p0 = piece * some_pairs
        chosen = []
        start = at_row[0]
        for w in range(w0, w0 + some):
            offset = offset_ref[first_window + w]
            other = packed[pl.ds(pl.multiple_of(start, 8), WIN), :]
            chosen.append(jnp.where(position >= offset, x_ref[w * WIN:w * WIN + WIN, :].astype(F32), other))
            start = start + sent(offset)
        at_row[0] = start
        normed = norm_rows(jnp.concatenate(chosen, axis=0), gain_ref[...])
        keys = dot_nt(wkt_ref[...], normed)
        values = dot(normed, wv_ref[...]).astype(BF)
        for half in range(2):
            for b in range(2):
                lo = half * 128 + b * 64
                for p in range(some_pairs):
                    pair = keys[lo:lo + 64, p * 128:p * 128 + 128]
                    turn = pltpu.roll(pair, WIN, 1)
                    to = (half, slice(b * 64, b * 64 + 64), slice(b * 128, b * 128 + 128))
                    w = w0 + 2 * p
                    kbd[(w,) + to] = jnp.where(block, jnp.where(first_lanes, pair, turn), 0.0).astype(BF)
                    kbd[(w + 1,) + to] = jnp.where(block, jnp.where(first_lanes, turn, pair), 0.0).astype(BF)
            for k in range(HALF):
                for w in range(some):
                    vbd[w0 + w, half, k * WIN:k * WIN + WIN, 0:128] = (
                        values[w * WIN:w * WIN + WIN, half * 128:half * 128 + 128] * lanes_of(k)
                    )

        wide = some_pairs * 128
        rows_s = some * SEAM
        seam_in = seam_ref[piece * rows_s:piece * rows_s + rows_s, :]
        seam_k = dot_nt(wkt_ref[...], seam_in).astype(BF)
        column = lax.broadcasted_iota(jnp.int32, (rows_s, wide), 1)
        spread = jnp.where(
            lax.broadcasted_iota(jnp.int32, (rows_s, wide), 0) == column // 128 * near + column % near, 1.0, 0.0
        ).astype(BF)
        of_head = (lax.broadcasted_iota(jnp.int32, (C, wide), 1) % 128) // near == (
            lax.broadcasted_iota(jnp.int32, (C, wide), 0) // DIM
        )
        seam_kt = jnp.where(of_head, dot(seam_k, spread), 0.0).astype(BF)
        seam_v = dot(seam_in, wv_ref[...]).astype(BF)
        for p in range(some_pairs):
            ksm[p0 + p] = seam_kt[:, p * 128:p * 128 + 128]
            for h in range(HEADS):
                half, k = h // HALF, h % HALF
                vsm[p0 + p, h * near:h * near + near, half * C:half * C + 128] = (
                    seam_v[p * near:p * near + near, half * 128:half * 128 + 128] * lanes_of(k)
                )

    def window_scores(w, half):
        at = pl.ds(pl.multiple_of(w * WIN, WIN), WIN)
        return dot(q_ref[at, half * 128:half * 128 + 128], kbd[w, half])

    def seam_scores(p):
        return dot(q_ref[pl.ds(pl.multiple_of(p * 128, 128), 128), :], ksm[p])

    def weigh(piece):
        pairs_here = range(piece * some_pairs, piece * some_pairs + some_pairs)
        windows_here = range(piece * some, piece * some + some)
        weights_s = [jnp.where(own, exp2(seam_scores(p)), 0.0).astype(BF) for p in pairs_here]
        weights_w = [[exp2(window_scores(w, half)).astype(BF) for half in range(2)] for w in windows_here]
        return weights_s, weights_w

    def add_up(piece, weights):
        weights_s, weights_w = weights
        for p in range(some_pairs):
            at = slice((piece * some_pairs + p) * 128, (piece * some_pairs + p) * 128 + 128)
            sums[at, :] = acc_ref[at, :] + dot(weights_s[p], vsm[piece * some_pairs + p])
        for w in range(some):
            at = slice((piece * some + w) * WIN, (piece * some + w) * WIN + WIN)
            for half in range(2):
                sums[at, half * C:half * C + C] += dot(weights_w[w][half], vbd[piece * some + w, half])

    def finish(piece):
        size = some * WIN
        at = slice(piece * size, piece * size + size)
        check = jnp.zeros((8, 128), F32)
        parts = []
        for half in range(2):
            den = sums[at, half * C + 128:half * C + C]
            inverse = 1.0 / den
            check = check + jnp.sum((den + inverse).reshape(size // 8, 8, 128), axis=0)
            parts.append(sums[at, half * C:half * C + 128] * inverse)
        attended = jnp.concatenate(parts, axis=1).astype(BF)
        out_ref[at, :] = (x_ref[at, :].astype(F32) + dot(attended, wo_ref[...])).astype(BF)
        return check

    build(0)
    check = jnp.zeros((8, 128), F32)
    for piece in range(PIECES):
        weights = weigh(piece)
        if piece + 1 < PIECES:
            build(piece + 1)
        add_up(piece, weights)
        if piece > 0:
            check = check + finish(piece - 1)
    check = check + finish(PIECES - 1)
    fine = jnp.sum(check) <= HIGH

    @pl.when(jnp.logical_not(fine))
    def _():
        copies = [pltpu.make_async_copy(kt_hbm, kt_ref, done.at[0]), pltpu.make_async_copy(vo_hbm, vo_ref, done.at[1])]
        for copy in copies:
            copy.start()
        for copy in copies:
            copy.wait()
        keys_g = kt_ref.shape[2]
        head_s = lax.broadcasted_iota(jnp.int32, (128, 128), 1) // near
        head_w = lax.broadcasted_iota(jnp.int32, (128, C), 1) // WIN

        def exact(p, carry):
            at = pl.ds(pl.multiple_of(p * 128, 128), 128)
            scores_s = jnp.where(own, seam_scores(p), NEG)
            tops_s = jnp.zeros((128, 128), F32)
            totals = []
            for half in range(2):
                q = q_ref[at, half * 128:half * 128 + 128]
                scores_w = jnp.concatenate([window_scores(2 * p + w, half) for w in range(2)], axis=0)
                tops_w = jnp.zeros((128, C), F32)
                total = jnp.zeros((128, C), F32)
                for k in range(HALF):
                    h = half * HALF + k
                    scores_g = dot(q, kt_ref[h])
                    top = jnp.max(scores_g, axis=1, keepdims=True)
                    top = jnp.maximum(top, jnp.max(jnp.where(head_s == h, scores_s, NEG), axis=1, keepdims=True))
                    top = jnp.maximum(top, jnp.max(jnp.where(head_w == k, scores_w, NEG), axis=1, keepdims=True))
                    tops_s = jnp.where(head_s == h, top, tops_s)
                    tops_w = jnp.where(head_w == k, top, tops_w)
                    total = total + dot(
                        exp2(scores_g - top).astype(BF), vo_ref[half, k * keys_g:k * keys_g + keys_g]
                    )
                weights = exp2(scores_w - tops_w).astype(BF)
                totals.append(total + jnp.concatenate(
                    [dot(weights[w * WIN:w * WIN + WIN], vbd[2 * p + w, half]) for w in range(2)], axis=0
                ))
            weights = jnp.where(own, exp2(jnp.where(own, scores_s - tops_s, NEG)), 0.0).astype(BF)
            total = jnp.concatenate(totals, axis=1) + dot(weights, vsm[p])
            again = jnp.concatenate(
                [total[:, half * C:half * C + 128] / total[:, half * C + 128:half * C + C] for half in range(2)], axis=1
            ).astype(BF)
            out_ref[at, :] = (x_ref[at, :].astype(F32) + dot(again, wo_ref[...])).astype(BF)
            return carry

        lax.fori_loop(0, pairs, exact, 0)


def window(offsets, x, main, rest, q, acc, seam_rows, gain, w_qkv, wo, kt, vo, rows=1024):
    pixels = x.shape[0]
    count = rows // WIN
    row = lambda i, s: (i, 0)
    fixed = lambda i, s: (0, 0)
    return pl.pallas_call(
        window_body,
        grid_spec=pltpu.PrefetchScalarGridSpec(
            num_scalar_prefetch=1,
            grid=(pixels // rows,),
            in_specs=[
                pl.BlockSpec((rows, C), row),
                pl.BlockSpec(main.shape, fixed),
                pl.BlockSpec(memory_space=pl.ANY),
                pl.BlockSpec((rows, C), row),
                pl.BlockSpec((rows, 2 * C), row),
                pl.BlockSpec((count * SEAM, C), row),
                pl.BlockSpec((1, C), fixed),
                pl.BlockSpec((C, C), lambda i, s: (0, 1)),
                pl.BlockSpec((C, C), lambda i, s: (0, 2)),
                pl.BlockSpec((C, C), fixed),
                pl.BlockSpec(memory_space=pl.ANY),
                pl.BlockSpec(memory_space=pl.ANY),
            ],
            out_specs=pl.BlockSpec((rows, C), row),
            scratch_shapes=[
                pltpu.VMEM((count, 2, 128, C), BF),
                pltpu.VMEM((count, 2, HALF * WIN, C), BF),
                pltpu.VMEM((count // 2, 128, 2 * C), BF),
                pltpu.VMEM((count // 2, C, 128), BF),
                pltpu.VMEM((rows, 2 * C), F32),
                pltpu.VMEM((pixels, C), F32),
                pltpu.VMEM(rest.shape, BF),
                pltpu.VMEM((C, C), BF),
                pltpu.VMEM(kt.shape, BF),
                pltpu.VMEM(vo.shape, BF),
                pltpu.SMEM((1,), jnp.int32),
                pltpu.SemaphoreType.DMA((2,)),
            ],
        ),
        out_shape=jax.ShapeDtypeStruct((pixels, C), BF),
        compiler_params=params(60),
        cost_estimate=pl.CostEstimate(
            flops=40 * pixels * C * C, bytes_accessed=20 * pixels * C, transcendentals=0
        ),
        name="window_attention",
    )(offsets, x, main, rest, q, acc, seam_rows, gain, w_qkv, w_qkv, wo, kt, vo)


def rotation(dx, dz, dy):
    pairs = []
    for f in range(32):
        x, z, y = f // 8, f // 4 % 2, f % 4
        pairs.append((f, (x + dx) % 4 * 8 + (z + dz) % 2 * 4 + (y + dy) % 4))
    return pairs


def partner(x):
    return lax.ppermute(x, "face", [(i, i ^ 1) for i in range(32)])


def turned(block, steps):
    return [block] + [lax.ppermute(block, "face", rotation(*s)) for s in steps]


def place_in_pool(index, windows):
    face, local = index // windows, index % windows
    me = lax.axis_index("face")
    dx = (me // 8 - face // 8) % 4
    dz = (me // 4 - face // 4) % 2
    dy = (me - face) % 4
    return ((dx * 2 + dz) * 4 + dy) * windows + local


def by_sub(x, k):
    return lax.ppermute(x, "sub", [(i, i ^ k) for i in range(4)])


def local(pixel_state, norm1_gain, w_qkv, w_out, shift_offsets, seam_table):
    pixels = pixel_state.shape[0]
    gain = norm1_gain.reshape(1, C)
    asked = partner(shift_offsets)
    pooled, asked = lax.optimization_barrier((pool_rows(pixel_state, gain), asked))
    groups = [pooled] + [by_sub(pooled, k) for k in (1, 2, 3)]
    columns = turned(pooled, [(0, 0, 1), (0, 0, 2), (0, 0, 3)])
    main, rest, more = pack(asked, shift_offsets, pixel_state)
    main = partner(main)
    planes = turned(join(*columns), [(0, 1, 0)])
    cube = join(*planes)
    pools = turned(cube, [(1, 0, 0), (2, 0, 0), (3, 0, 0)])
    kt, vo = group(groups, w_qkv)
    split = pixels // 4
    sums = coarse(0, split, pixel_state, gain, w_qkv, kt, vo, gain, rows=512)
    q, acc = coarse(split, pixels - split, pixel_state, gain, w_qkv, kt, vo, cube, sums)
    index = place_in_pool(seam_table, pooled.shape[0]).reshape(-1, 1)
    seam_rows = seam(index, pools)
    _, rest = lax.while_loop(lambda c: c[0] > 0, lambda c: (c[0] - 1, partner(c[1])), (more[0], rest))
    return window(shift_offsets, pixel_state, main, rest, q, acc, seam_rows, gain, w_qkv, w_out, kt, vo)


def solution(mesh):
    return jax.shard_map(
        local,
        mesh=mesh,
        in_specs=(
            P(("face", "sub"), None),
            P(),
            P(),
            P(),
            P(("face", "sub")),
            P(("face", "sub"), None),
        ),
        out_specs=P(("face", "sub"), None),
        check_vma=False,
    )
```

```python
import functools
import math

import jax
import jax.numpy as jnp
from jax import lax
from jax.experimental import pallas as pl
from jax.experimental.pallas import tpu as pltpu
from jax.sharding import PartitionSpec as P

HEADS = 8
HALF = HEADS // 2
DIM = 32
C = 256
WIN = 64
SEAM = 8
EPS = 1e-05
SCALE = math.log2(math.e) / math.sqrt(DIM)
BF = jnp.bfloat16
F32 = jnp.float32
HIGH = 2.0 ** 100
NEG = -1e30
MB = 1024 * 1024
LIMIT = 5360
PIECES = 2


def params(limit):
    return pltpu.CompilerParams(vmem_limit_bytes=limit * MB)


def exp2(x):
    return jnp.exp2(x)


def dot(a, b):
    return jnp.dot(a, b, preferred_element_type=F32)


def dot_nt(a, b):
    return lax.dot_general(a, b, (((1,), (1,)), ((), ())), preferred_element_type=F32)


def sent(offset):
    return (offset + 7) // 8 * 8


def norm_rows(x, gain):
    centre = jnp.mean(x, axis=-1, keepdims=True)
    x = x - centre
    spread = jnp.mean(x * x, axis=-1, keepdims=True)
    return (x * lax.rsqrt(spread + EPS) * gain).astype(BF)


def pool_body(x_ref, gain_ref, pooled_ref):
    rows = x_ref.shape[0]
    normed = norm_rows(x_ref[...].astype(F32), gain_ref[...])
    count = rows // WIN
    row = lax.broadcasted_iota(jnp.int32, (count, rows), 1) // WIN
    pick = jnp.where(row == lax.broadcasted_iota(jnp.int32, (count, rows), 0), 1.0, 0.0).astype(BF)
    pooled_ref[...] = (dot(pick, normed) * (1.0 / math.sqrt(WIN))).astype(BF)


def pool_rows(x, gain, rows=2048):
    pixels = x.shape[0]
    return pl.pallas_call(
        pool_body,
        grid=(pixels // rows,),
        in_specs=[
            pl.BlockSpec((rows, C), lambda i: (i, 0)),
            pl.BlockSpec((1, C), lambda i: (0, 0)),
        ],
        out_specs=pl.BlockSpec((rows // WIN, C), lambda i: (i, 0)),
        out_shape=jax.ShapeDtypeStruct((pixels // WIN, C), BF),
        compiler_params=params(60),
        cost_estimate=pl.CostEstimate(flops=2 * pixels * C * C, bytes_accessed=4 * pixels * C, transcendentals=0),
        name="norm_pool",
    )(x, gain)


def pack_body(offset_ref, mine_ref, x_ref, main_ref, rest_ref, more_ref, packed, at_row):
    step = pl.program_id(0)
    count = x_ref.shape[0] // WIN
    @pl.when(step == 0)
    def _():
        at_row[0] = 0

    start = at_row[0]
    for w in range(count):
        packed[pl.ds(pl.multiple_of(start, 8), WIN), :] = x_ref[w * WIN:w * WIN + WIN, :].astype(F32)
        start = start + sent(offset_ref[step * count + w])
    at_row[0] = start

    @pl.when(step == pl.num_programs(0) - 1)
    def _():
        main_ref[...] = packed[0:LIMIT, :].astype(BF)
        mine = lax.fori_loop(0, mine_ref.shape[0], lambda w, total: total + sent(mine_ref[w]), 0)
        more_ref[0] = (jnp.maximum(start, mine) > LIMIT).astype(jnp.int32)

        @pl.when(start > LIMIT)
        def _():
            rest_ref[...] = packed[LIMIT:, :].astype(BF)


def pack(offsets, mine, x, rows=4096):
    pixels = x.shape[0]
    whole = lambda i, s, t: (0, 0)
    return pl.pallas_call(
        pack_body,
        grid_spec=pltpu.PrefetchScalarGridSpec(
            num_scalar_prefetch=2,
            grid=(pixels // rows,),
            in_specs=[pl.BlockSpec((rows, C), lambda i, s, t: (i, 0))],
            out_specs=[
                pl.BlockSpec((LIMIT, C), whole),
                pl.BlockSpec((pixels - LIMIT, C), whole),
                pl.BlockSpec(memory_space=pltpu.SMEM),
            ],
            scratch_shapes=[pltpu.VMEM((pixels, C), F32), pltpu.SMEM((1,), jnp.int32)],
        ),
        out_shape=[
            jax.ShapeDtypeStruct((LIMIT, C), BF),
            jax.ShapeDtypeStruct((pixels - LIMIT, C), BF),
            jax.ShapeDtypeStruct((1,), jnp.int32),
        ],
        compiler_params=params(60),
        cost_estimate=pl.CostEstimate(flops=0, bytes_accessed=10 * pixels * C, transcendentals=0),
        name="pack_rows",
    )(offsets, mine, x)


def join_body(*refs):
    lo = 0
    for ref in refs[:-1]:
        refs[-1][lo:lo + ref.shape[0]] = ref[...]
        lo += ref.shape[0]


def join(*blocks):
    rows = sum(b.shape[0] for b in blocks)
    return pl.pallas_call(
        join_body, out_shape=jax.ShapeDtypeStruct((rows, C), BF), compiler_params=params(32), name="join_blocks"
    )(*blocks)


def lay_out_group(blocks, wk_ref, wv_ref, kt_ref, vo_ref):
    g = jnp.concatenate([ref[...] for ref in blocks], axis=0)
    count = g.shape[0]
    kt = lax.dot_general(wk_ref[...], g, (((0,), (1,)), ((), ())), preferred_element_type=F32)
    v = dot(g, wv_ref[...])
    feat = lax.broadcasted_iota(jnp.int32, (128, count), 0) // DIM
    lane = lax.broadcasted_iota(jnp.int32, (count, 128), 1) // DIM
    for h in range(HEADS):
        half, k = h // HALF, h % HALF
        kt_ref[h] = jnp.where(feat == k, kt[half * 128:half * 128 + 128], 0.0).astype(BF)
        vo_ref[half, k * count:k * count + count, 0:128] = jnp.where(
            lane == k, v[:, half * 128:half * 128 + 128], 0.0
        ).astype(BF)
        vo_ref[half, k * count:k * count + count, 128:256] = jnp.where(lane == k, 1.0, 0.0).astype(BF)


def group_scratch(blocks):
    count = sum(b.shape[0] for b in blocks)
    return [pltpu.VMEM((HEADS, 128, count), BF), pltpu.VMEM((2, HALF * count, C), BF)]


def coarse_body(blocks, x_ref, next_ref, gain_ref, wq_ref, wk_ref, wv_ref, *refs):
    q_ref, acc_ref, held, kt_ref, vo_ref = refs[-5:]
    step = pl.program_id(0)

    def queries(ref):
        return (dot(norm_rows(ref[...].astype(F32), gain_ref[...]), wq_ref[...]) * SCALE).astype(BF)

    @pl.when(step == 0)
    def _():
        lay_out_group(refs[:blocks], wk_ref, wv_ref, kt_ref, vo_ref)
        held[...] = queries(x_ref)

    q = held[...]
    q_ref[...] = q
    weights = []
    for half in range(2):
        heads = range(half * HALF, half * HALF + HALF)
        mine = q[:, half * 128:half * 128 + 128]
        weights.append(jnp.concatenate([exp2(dot(mine, kt_ref[h])).astype(BF) for h in heads], axis=1))
    acc_ref[:, 0:C] = dot(weights[0], vo_ref[0])
    acc_ref[:, C:2 * C] = dot(weights[1], vo_ref[1])
    held[...] = queries(next_ref)


def coarse(first, run, x, gain, w_qkv, blocks, after, given=(), rows=1024):
    pixels = x.shape[0]
    steps = run // rows
    base = first // rows
    count = sum(b.shape[0] for b in blocks)
    fixed = 6 + len(blocks) + 1
    return pl.pallas_call(
        functools.partial(coarse_body, len(blocks)),
        grid=(steps,),
        in_specs=[
            pl.BlockSpec((rows, C), lambda i: (base, 0)),
            pl.BlockSpec((rows, C), lambda i: (base + jnp.minimum(i + 1, steps - 1), 0)),
            pl.BlockSpec((1, C), lambda i: (0, 0)),
            pl.BlockSpec((C, C), lambda i: (0, 0)),
            pl.BlockSpec((C, C), lambda i: (0, 1)),
            pl.BlockSpec((C, C), lambda i: (0, 2)),
        ]
        + [pl.BlockSpec(b.shape, lambda i: (0, 0)) for b in blocks]
        + [pl.BlockSpec(memory_space=pl.ANY)] * (1 + len(given)),
        out_specs=[
            pl.BlockSpec((rows, C), lambda i: (base + i, 0)),
            pl.BlockSpec((rows, 2 * C), lambda i: (base + i, 0)),
        ],
        out_shape=[
            jax.ShapeDtypeStruct((pixels, C), BF),
            jax.ShapeDtypeStruct((pixels, 2 * C), F32),
        ],
        scratch_shapes=[pltpu.VMEM((rows, C), BF)] + group_scratch(blocks),
        input_output_aliases={fixed: 0, fixed + 1: 1} if given else {},
        compiler_params=params(60),
        cost_estimate=pl.CostEstimate(
            flops=4 * run * HEADS * count * C, bytes_accessed=10 * run * C, transcendentals=run * HEADS * count
        ),
        name="group_attention",
    )(x, x, gain, w_qkv, w_qkv, w_qkv, *blocks, after, *given)


def seam_body(index_ref, *refs):
    out_ref = refs[-1]
    rows = index_ref.shape[0]
    total = jnp.zeros((rows, C), F32)
    lo = 0
    for ref in refs[:-1]:
        step = ref.shape[0]
        at = lax.broadcasted_iota(jnp.int32, (rows, step), 1) + lo
        pick = jnp.where(at == index_ref[...], 1.0, 0.0).astype(BF)
        total = total + dot(pick, ref[...])
        lo += step
    out_ref[...] = total.astype(BF)


def seam(index, pools, rows=256):
    count = index.shape[0]
    return pl.pallas_call(
        seam_body,
        grid=(count // rows,),
        in_specs=[pl.BlockSpec((rows, 1), lambda i: (i, 0))]
        + [pl.BlockSpec(pool.shape, lambda i: (0, 0)) for pool in pools],
        out_specs=pl.BlockSpec((rows, C), lambda i: (i, 0)),
        out_shape=jax.ShapeDtypeStruct((count, C), BF),
        compiler_params=params(48),
        name="seam_rows",
    )(index, *pools)


def window_body(
    offset_ref, x_ref, main_ref, rest_hbm, q_ref, acc_ref, seam_ref, gain_ref, wk_ref, wv_ref, wo_ref, *refs,
):
    out_ref, kbd, vbd, vsm, ksm, mixed, packed, rest_ref, wkt_ref, kt_ref, vo_ref, at_row, done = refs[-13:]
    blocks = refs[:-13]
    rows = x_ref.shape[0]
    count = rows // WIN
    pairs = count // 2
    near = 2 * SEAM
    step = pl.program_id(0)
    first_window = step * count

    def lanes_of(k):
        return jnp.where(lax.broadcasted_iota(jnp.int32, (1, 128), 1) // DIM == k, 1.0, 0.0).astype(BF)

    position = lax.broadcasted_iota(jnp.int32, (WIN, 1), 0)

    @pl.when(step == 0)
    def _():
        at_row[0] = 0
        wkt_ref[...] = wk_ref[...].astype(F32).T.astype(BF)
        packed[0:LIMIT, :] = main_ref[...].astype(F32)

        def add(w, total):
            return total + sent(offset_ref[w])

        @pl.when(lax.fori_loop(0, pl.num_programs(0) * count, add, 0) > LIMIT)
        def _():
            copy = pltpu.make_async_copy(rest_hbm, rest_ref, done)
            copy.start()
            copy.wait()
            packed[LIMIT:, :] = rest_ref[...].astype(F32)

        kbd[...] = jnp.zeros(kbd.shape, BF)
        vsm[...] = jnp.zeros(vsm.shape, BF)
        for half in range(2):
            for k in range(HALF):
                for w in range(count):
                    vbd[w, half, k * WIN:k * WIN + WIN, 128:256] = jnp.broadcast_to(lanes_of(k), (WIN, 128))
                h = half * HALF + k
                for p in range(pairs):
                    vsm[p, h * near:h * near + near, half * C + 128:half * C + C] = jnp.broadcast_to(
                        lanes_of(k), (near, 128)
                    )

    block = (lax.broadcasted_iota(jnp.int32, (64, 128), 0) // DIM) == (
        lax.broadcasted_iota(jnp.int32, (64, 128), 1) // WIN
    )
    first_lanes = lax.broadcasted_iota(jnp.int32, (64, 128), 1) < WIN
    own = (lax.broadcasted_iota(jnp.int32, (128, 128), 1) % near) // SEAM == (
        lax.broadcasted_iota(jnp.int32, (128, 128), 0) // WIN
    )
    some = count // PIECES
    some_pairs = some // 2

    def build(piece):
        w0 = piece * some
        p0 = piece * some_pairs
        chosen = []
        start = at_row[0]
        for w in range(w0, w0 + some):
            offset = offset_ref[first_window + w]
            other = packed[pl.ds(pl.multiple_of(start, 8), WIN), :]
            chosen.append(jnp.where(position >= offset, x_ref[w * WIN:w * WIN + WIN, :].astype(F32), other))
            start = start + sent(offset)
        at_row[0] = start
        normed = norm_rows(jnp.concatenate(chosen, axis=0), gain_ref[...])
        keys = dot_nt(wkt_ref[...], normed)
        values = dot(normed, wv_ref[...]).astype(BF)
        for half in range(2):
            for b in range(2):
                lo = half * 128 + b * 64
                for p in range(some_pairs):
                    pair = keys[lo:lo + 64, p * 128:p * 128 + 128]
                    turn = pltpu.roll(pair, WIN, 1)
                    to = (half, slice(b * 64, b * 64 + 64), slice(b * 128, b * 128 + 128))
                    w = w0 + 2 * p
                    kbd[(w,) + to] = jnp.where(block, jnp.where(first_lanes, pair, turn), 0.0).astype(BF)
                    kbd[(w + 1,) + to] = jnp.where(block, jnp.where(first_lanes, turn, pair), 0.0).astype(BF)
            for k in range(HALF):
                for w in range(some):
                    vbd[w0 + w, half, k * WIN:k * WIN + WIN, 0:128] = (
                        values[w * WIN:w * WIN + WIN, half * 128:half * 128 + 128] * lanes_of(k)
                    )

        wide = some_pairs * 128
        rows_s = some * SEAM
        seam_in = seam_ref[piece * rows_s:piece * rows_s + rows_s, :]
        seam_k = dot_nt(wkt_ref[...], seam_in).astype(BF)
        column = lax.broadcasted_iota(jnp.int32, (rows_s, wide), 1)
        spread = jnp.where(
            lax.broadcasted_iota(jnp.int32, (rows_s, wide), 0) == column // 128 * near + column % near, 1.0, 0.0
        ).astype(BF)
        of_head = (lax.broadcasted_iota(jnp.int32, (C, wide), 1) % 128) // near == (
            lax.broadcasted_iota(jnp.int32, (C, wide), 0) // DIM
        )
        seam_kt = jnp.where(of_head, dot(seam_k, spread), 0.0).astype(BF)
        seam_v = dot(seam_in, wv_ref[...]).astype(BF)
        for p in range(some_pairs):
            ksm[p0 + p] = seam_kt[:, p * 128:p * 128 + 128]
            for h in range(HEADS):
                half, k = h // HALF, h % HALF
                vsm[p0 + p, h * near:h * near + near, half * C:half * C + 128] = (
                    seam_v[p * near:p * near + near, half * 128:half * 128 + 128] * lanes_of(k)
                )

    def window_scores(w, half):
        at = pl.ds(pl.multiple_of(w * WIN, WIN), WIN)
        return dot(q_ref[at, half * 128:half * 128 + 128], kbd[w, half])

    def seam_scores(p):
        return dot(q_ref[pl.ds(pl.multiple_of(p * 128, 128), 128), :], ksm[p])

    def weigh(piece):
        pairs_here = range(piece * some_pairs, piece * some_pairs + some_pairs)
        windows_here = range(piece * some, piece * some + some)
        weights_s = [jnp.where(own, exp2(seam_scores(p)), 0.0).astype(BF) for p in pairs_here]
        weights_w = [[exp2(window_scores(w, half)).astype(BF) for half in range(2)] for w in windows_here]
        return weights_s, weights_w

    def add_up(piece, weights):
        weights_s, weights_w = weights
        check = jnp.zeros((8, 128), F32)
        for p in range(some_pairs):
            lo = (piece * some_pairs + p) * 128
            base = acc_ref[lo:lo + 128, :] + dot(weights_s[p], vsm[piece * some_pairs + p])
            for half in range(2):
                total = base[:, half * C:half * C + C] + jnp.concatenate(
                    [dot(weights_w[2 * p + w][half], vbd[piece * some + 2 * p + w, half]) for w in range(2)], axis=0
                )
                den = total[:, 128:256]
                inverse = 1.0 / den
                check = check + jnp.sum((den + inverse).reshape(16, 8, 128), axis=0)
                mixed[lo:lo + 128, half * 128:half * 128 + 128] = (total[:, 0:128] * inverse).astype(BF)
        return check

    def finish(piece):
        at = slice(piece * some * WIN, piece * some * WIN + some * WIN)
        out_ref[at, :] = (x_ref[at, :].astype(F32) + dot(mixed[at, :], wo_ref[...])).astype(BF)

    build(0)
    check = jnp.zeros((8, 128), F32)
    for piece in range(PIECES):
        weights = weigh(piece)
        if piece + 1 < PIECES:
            build(piece + 1)
        check = check + add_up(piece, weights)
        if piece > 0:
            finish(piece - 1)
    finish(PIECES - 1)
    fine = jnp.sum(check) <= HIGH

    @pl.when(jnp.logical_not(fine))
    def _():
        lay_out_group(blocks, wk_ref, wv_ref, kt_ref, vo_ref)
        keys_g = kt_ref.shape[2]
        head_s = lax.broadcasted_iota(jnp.int32, (128, 128), 1) // near
        head_w = lax.broadcasted_iota(jnp.int32, (128, C), 1) // WIN

        def exact(p, carry):
            at = pl.ds(pl.multiple_of(p * 128, 128), 128)
            scores_s = jnp.where(own, seam_scores(p), NEG)
            tops_s = jnp.zeros((128, 128), F32)
            totals = []
            for half in range(2):
                q = q_ref[at, half * 128:half * 128 + 128]
                scores_w = jnp.concatenate([window_scores(2 * p + w, half) for w in range(2)], axis=0)
                tops_w = jnp.zeros((128, C), F32)
                total = jnp.zeros((128, C), F32)
                for k in range(HALF):
                    h = half * HALF + k
                    scores_g = dot(q, kt_ref[h])
                    top = jnp.max(scores_g, axis=1, keepdims=True)
                    top = jnp.maximum(top, jnp.max(jnp.where(head_s == h, scores_s, NEG), axis=1, keepdims=True))
                    top = jnp.maximum(top, jnp.max(jnp.where(head_w == k, scores_w, NEG), axis=1, keepdims=True))
                    tops_s = jnp.where(head_s == h, top, tops_s)
                    tops_w = jnp.where(head_w == k, top, tops_w)
                    total = total + dot(
                        exp2(scores_g - top).astype(BF), vo_ref[half, k * keys_g:k * keys_g + keys_g]
                    )
                weights = exp2(scores_w - tops_w).astype(BF)
                totals.append(total + jnp.concatenate(
                    [dot(weights[w * WIN:w * WIN + WIN], vbd[2 * p + w, half]) for w in range(2)], axis=0
                ))
            weights = jnp.where(own, exp2(jnp.where(own, scores_s - tops_s, NEG)), 0.0).astype(BF)
            total = jnp.concatenate(totals, axis=1) + dot(weights, vsm[p])
            again = jnp.concatenate(
                [total[:, half * C:half * C + 128] / total[:, half * C + 128:half * C + C] for half in range(2)], axis=1
            ).astype(BF)
            out_ref[at, :] = (x_ref[at, :].astype(F32) + dot(again, wo_ref[...])).astype(BF)
            return carry

        lax.fori_loop(0, pairs, exact, 0)


def window(offsets, x, main, rest, q, acc, seam_rows, gain, w_qkv, wo, blocks, rows=1024):
    pixels = x.shape[0]
    count = rows // WIN
    row = lambda i, s: (i, 0)
    fixed = lambda i, s: (0, 0)
    return pl.pallas_call(
        window_body,
        grid_spec=pltpu.PrefetchScalarGridSpec(
            num_scalar_prefetch=1,
            grid=(pixels // rows,),
            in_specs=[
                pl.BlockSpec((rows, C), row),
                pl.BlockSpec(main.shape, fixed),
                pl.BlockSpec(memory_space=pl.ANY),
                pl.BlockSpec((rows, C), row),
                pl.BlockSpec((rows, 2 * C), row),
                pl.BlockSpec((count * SEAM, C), row),
                pl.BlockSpec((1, C), fixed),
                pl.BlockSpec((C, C), lambda i, s: (0, 1)),
                pl.BlockSpec((C, C), lambda i, s: (0, 2)),
                pl.BlockSpec((C, C), fixed),
            ]
            + [pl.BlockSpec(b.shape, fixed) for b in blocks],
            out_specs=pl.BlockSpec((rows, C), row),
            scratch_shapes=[
                pltpu.VMEM((count, 2, 128, C), BF),
                pltpu.VMEM((count, 2, HALF * WIN, C), BF),
                pltpu.VMEM((count // 2, 128, 2 * C), BF),
                pltpu.VMEM((count // 2, C, 128), BF),
                pltpu.VMEM((rows, C), BF),
                pltpu.VMEM((pixels, C), F32),
                pltpu.VMEM(rest.shape, BF),
                pltpu.VMEM((C, C), BF),
                *group_scratch(blocks),
                pltpu.SMEM((1,), jnp.int32),
                pltpu.SemaphoreType.DMA,
            ],
        ),
        out_shape=jax.ShapeDtypeStruct((pixels, C), BF),
        compiler_params=params(60),
        cost_estimate=pl.CostEstimate(
            flops=40 * pixels * C * C, bytes_accessed=20 * pixels * C, transcendentals=0
        ),
        name="window_attention",
    )(offsets, x, main, rest, q, acc, seam_rows, gain, w_qkv, w_qkv, wo, *blocks)


def rotation(dx, dz, dy):
    pairs = []
    for f in range(32):
        x, z, y = f // 8, f // 4 % 2, f % 4
        pairs.append((f, (x + dx) % 4 * 8 + (z + dz) % 2 * 4 + (y + dy) % 4))
    return pairs


def partner(x):
    return lax.ppermute(x, "face", [(i, i ^ 1) for i in range(32)])


def turned(block, steps):
    return [block] + [lax.ppermute(block, "face", rotation(*s)) for s in steps]


def place_in_pool(index, windows):
    face, local = index // windows, index % windows
    me = lax.axis_index("face")
    dx = (me // 8 - face // 8) % 4
    dz = (me // 4 - face // 4) % 2
    dy = (me - face) % 4
    return ((dx * 2 + dz) * 4 + dy) * windows + local


def by_sub(x, k):
    return lax.ppermute(x, "sub", [(i, i ^ k) for i in range(4)])


def local(pixel_state, norm1_gain, w_qkv, w_out, shift_offsets, seam_table):
    pixels = pixel_state.shape[0]
    gain = norm1_gain.reshape(1, C)
    asked = partner(shift_offsets)
    pooled, asked = lax.optimization_barrier((pool_rows(pixel_state, gain), asked))
    groups = [pooled] + [by_sub(pooled, k) for k in (1, 2, 3)]
    columns = turned(pooled, [(0, 0, 1), (0, 0, 2), (0, 0, 3)])
    main, rest, more = pack(asked, shift_offsets, pixel_state)
    main = partner(main)
    planes = turned(join(*columns), [(0, 1, 0)])
    cube = join(*planes)
    pools = turned(cube, [(1, 0, 0), (2, 0, 0), (3, 0, 0)])
    split = pixels // 4
    sums = coarse(0, split, pixel_state, gain, w_qkv, groups, gain, rows=512)
    q, acc = coarse(split, pixels - split, pixel_state, gain, w_qkv, groups, cube, sums)
    index = place_in_pool(seam_table, pooled.shape[0]).reshape(-1, 1)
    seam_rows = seam(index, pools)
    _, rest = lax.while_loop(lambda c: c[0] > 0, lambda c: (c[0] - 1, partner(c[1])), (more[0], rest))
    return window(shift_offsets, pixel_state, main, rest, q, acc, seam_rows, gain, w_qkv, w_out, groups)


def solution(mesh):
    return jax.shard_map(
        local,
        mesh=mesh,
        in_specs=(
            P(("face", "sub"), None),
            P(),
            P(),
            P(),
            P(("face", "sub")),
            P(("face", "sub"), None),
        ),
        out_specs=P(("face", "sub"), None),
        check_vma=False,
    )
```

```python
import functools
import math

import jax
import jax.numpy as jnp
from jax import lax
from jax.experimental import pallas as pl
from jax.experimental.pallas import tpu as pltpu
from jax.sharding import PartitionSpec as P

HEADS = 8
HALF = HEADS // 2
DIM = 32
C = 256
WIN = 64
SEAM = 8
EPS = 1e-05
SCALE = math.log2(math.e) / math.sqrt(DIM)
BF = jnp.bfloat16
F32 = jnp.float32
HIGH = 2.0 ** 100
NEG = -1e30
MB = 1024 * 1024
LIMIT = 5360
PIECES = 2


def params(limit):
    return pltpu.CompilerParams(vmem_limit_bytes=limit * MB)


def exp2(x):
    return jnp.exp2(x)


def dot(a, b):
    return jnp.dot(a, b, preferred_element_type=F32)


def dot_nt(a, b):
    return lax.dot_general(a, b, (((1,), (1,)), ((), ())), preferred_element_type=F32)


def sent(offset):
    return (offset + 7) // 8 * 8


def norm_rows(x, gain):
    centre = jnp.mean(x, axis=-1, keepdims=True)
    x = x - centre
    spread = jnp.mean(x * x, axis=-1, keepdims=True)
    return (x * lax.rsqrt(spread + EPS) * gain).astype(BF)


def pool_body(x_ref, gain_ref, pooled_ref):
    rows = x_ref.shape[0]
    normed = norm_rows(x_ref[...].astype(F32), gain_ref[...])
    count = rows // WIN
    row = lax.broadcasted_iota(jnp.int32, (count, rows), 1) // WIN
    pick = jnp.where(row == lax.broadcasted_iota(jnp.int32, (count, rows), 0), 1.0, 0.0).astype(BF)
    pooled_ref[...] = (dot(pick, normed) * (1.0 / math.sqrt(WIN))).astype(BF)


def pool_rows(x, gain, rows=2048):
    pixels = x.shape[0]
    return pl.pallas_call(
        pool_body,
        grid=(pixels // rows,),
        in_specs=[
            pl.BlockSpec((rows, C), lambda i: (i, 0)),
            pl.BlockSpec((1, C), lambda i: (0, 0)),
        ],
        out_specs=pl.BlockSpec((rows // WIN, C), lambda i: (i, 0)),
        out_shape=jax.ShapeDtypeStruct((pixels // WIN, C), BF),
        compiler_params=params(60),
        cost_estimate=pl.CostEstimate(flops=2 * pixels * C * C, bytes_accessed=4 * pixels * C, transcendentals=0),
        name="norm_pool",
    )(x, gain)


def pack_body(offset_ref, mine_ref, x_ref, main_ref, rest_hbm, more_ref, packed, rest_ref, at_row, done):
    step = pl.program_id(0)
    count = x_ref.shape[0] // WIN
    @pl.when(step == 0)
    def _():
        at_row[0] = 0

    start = at_row[0]
    for w in range(count):
        packed[pl.ds(pl.multiple_of(start, 8), WIN), :] = x_ref[w * WIN:w * WIN + WIN, :].astype(F32)
        start = start + sent(offset_ref[step * count + w])
    at_row[0] = start

    @pl.when(step == pl.num_programs(0) - 1)
    def _():
        main_ref[...] = packed[0:LIMIT, :].astype(BF)
        mine = lax.fori_loop(0, mine_ref.shape[0], lambda w, total: total + sent(mine_ref[w]), 0)
        more_ref[0] = (jnp.maximum(start, mine) > LIMIT).astype(jnp.int32)

        @pl.when(start > LIMIT)
        def _():
            rest_ref[...] = packed[LIMIT:, :].astype(BF)
            copy = pltpu.make_async_copy(rest_ref, rest_hbm, done)
            copy.start()
            copy.wait()


def pack(offsets, mine, x, rows=4096):
    pixels = x.shape[0]
    whole = lambda i, s, t: (0, 0)
    return pl.pallas_call(
        pack_body,
        grid_spec=pltpu.PrefetchScalarGridSpec(
            num_scalar_prefetch=2,
            grid=(pixels // rows,),
            in_specs=[pl.BlockSpec((rows, C), lambda i, s, t: (i, 0))],
            out_specs=[
                pl.BlockSpec((LIMIT, C), whole),
                pl.BlockSpec(memory_space=pl.ANY),
                pl.BlockSpec(memory_space=pltpu.SMEM),
            ],
            scratch_shapes=[
                pltpu.VMEM((pixels, C), F32),
                pltpu.VMEM((pixels - LIMIT, C), BF),
                pltpu.SMEM((1,), jnp.int32),
                pltpu.SemaphoreType.DMA,
            ],
        ),
        out_shape=[
            jax.ShapeDtypeStruct((LIMIT, C), BF),
            jax.ShapeDtypeStruct((pixels - LIMIT, C), BF),
            jax.ShapeDtypeStruct((1,), jnp.int32),
        ],
        compiler_params=params(60),
        cost_estimate=pl.CostEstimate(flops=0, bytes_accessed=10 * pixels * C, transcendentals=0),
        name="pack_rows",
    )(offsets, mine, x)


def join_body(*refs):
    lo = 0
    for ref in refs[:-1]:
        refs[-1][lo:lo + ref.shape[0]] = ref[...]
        lo += ref.shape[0]


def join(*blocks):
    rows = sum(b.shape[0] for b in blocks)
    return pl.pallas_call(
        join_body, out_shape=jax.ShapeDtypeStruct((rows, C), BF), compiler_params=params(32), name="join_blocks"
    )(*blocks)


def lay_out_group(blocks, wk_ref, wv_ref, kt_ref, vo_ref):
    g = jnp.concatenate([ref[...] for ref in blocks], axis=0)
    count = g.shape[0]
    kt = lax.dot_general(wk_ref[...], g, (((0,), (1,)), ((), ())), preferred_element_type=F32)
    v = dot(g, wv_ref[...])
    feat = lax.broadcasted_iota(jnp.int32, (128, count), 0) // DIM
    lane = lax.broadcasted_iota(jnp.int32, (count, 128), 1) // DIM
    for h in range(HEADS):
        half, k = h // HALF, h % HALF
        kt_ref[h] = jnp.where(feat == k, kt[half * 128:half * 128 + 128], 0.0).astype(BF)
        vo_ref[half, k * count:k * count + count, 0:128] = jnp.where(
            lane == k, v[:, half * 128:half * 128 + 128], 0.0
        ).astype(BF)
        vo_ref[half, k * count:k * count + count, 128:256] = jnp.where(lane == k, 1.0, 0.0).astype(BF)


def group_scratch(blocks):
    count = sum(b.shape[0] for b in blocks)
    return [pltpu.VMEM((HEADS, 128, count), BF), pltpu.VMEM((2, HALF * count, C), BF)]


def coarse_body(blocks, x_ref, next_ref, gain_ref, wq_ref, wk_ref, wv_ref, *refs):
    q_ref, acc_ref, held, kt_ref, vo_ref = refs[-5:]
    step = pl.program_id(0)

    def queries(ref):
        return (dot(norm_rows(ref[...].astype(F32), gain_ref[...]), wq_ref[...]) * SCALE).astype(BF)

    @pl.when(step == 0)
    def _():
        lay_out_group(refs[:blocks], wk_ref, wv_ref, kt_ref, vo_ref)
        held[...] = queries(x_ref)

    q = held[...]
    q_ref[...] = q
    weights = []
    for half in range(2):
        heads = range(half * HALF, half * HALF + HALF)
        mine = q[:, half * 128:half * 128 + 128]
        weights.append(jnp.concatenate([exp2(dot(mine, kt_ref[h])).astype(BF) for h in heads], axis=1))
    acc_ref[:, 0:C] = dot(weights[0], vo_ref[0])
    acc_ref[:, C:2 * C] = dot(weights[1], vo_ref[1])
    held[...] = queries(next_ref)


def coarse(first, run, x, gain, w_qkv, blocks, after, given=(), rows=1024):
    pixels = x.shape[0]
    steps = run // rows
    base = first // rows
    count = sum(b.shape[0] for b in blocks)
    fixed = 6 + len(blocks) + 1
    return pl.pallas_call(
        functools.partial(coarse_body, len(blocks)),
        grid=(steps,),
        in_specs=[
            pl.BlockSpec((rows, C), lambda i: (base, 0)),
            pl.BlockSpec((rows, C), lambda i: (base + jnp.minimum(i + 1, steps - 1), 0)),
            pl.BlockSpec((1, C), lambda i: (0, 0)),
            pl.BlockSpec((C, C), lambda i: (0, 0)),
            pl.BlockSpec((C, C), lambda i: (0, 1)),
            pl.BlockSpec((C, C), lambda i: (0, 2)),
        ]
        + [pl.BlockSpec(b.shape, lambda i: (0, 0)) for b in blocks]
        + [pl.BlockSpec(memory_space=pl.ANY)] * (1 + len(given)),
        out_specs=[
            pl.BlockSpec((rows, C), lambda i: (base + i, 0)),
            pl.BlockSpec((rows, 2 * C), lambda i: (base + i, 0)),
        ],
        out_shape=[
            jax.ShapeDtypeStruct((pixels, C), BF),
            jax.ShapeDtypeStruct((pixels, 2 * C), F32),
        ],
        scratch_shapes=[pltpu.VMEM((rows, C), BF)] + group_scratch(blocks),
        input_output_aliases={fixed: 0, fixed + 1: 1} if given else {},
        compiler_params=params(60),
        cost_estimate=pl.CostEstimate(
            flops=4 * run * HEADS * count * C, bytes_accessed=10 * run * C, transcendentals=run * HEADS * count
        ),
        name="group_attention",
    )(x, x, gain, w_qkv, w_qkv, w_qkv, *blocks, after, *given)


def seam_body(index_ref, *refs):
    out_ref = refs[-1]
    rows = index_ref.shape[0]
    total = jnp.zeros((rows, C), F32)
    lo = 0
    for ref in refs[:-1]:
        step = ref.shape[0]
        at = lax.broadcasted_iota(jnp.int32, (rows, step), 1) + lo
        pick = jnp.where(at == index_ref[...], 1.0, 0.0).astype(BF)
        total = total + dot(pick, ref[...])
        lo += step
    out_ref[...] = total.astype(BF)


def seam(index, pools, rows=256):
    count = index.shape[0]
    return pl.pallas_call(
        seam_body,
        grid=(count // rows,),
        in_specs=[pl.BlockSpec((rows, 1), lambda i: (i, 0))]
        + [pl.BlockSpec(pool.shape, lambda i: (0, 0)) for pool in pools],
        out_specs=pl.BlockSpec((rows, C), lambda i: (i, 0)),
        out_shape=jax.ShapeDtypeStruct((count, C), BF),
        compiler_params=params(48),
        name="seam_rows",
    )(index, *pools)


def window_body(
    offset_ref, x_ref, main_ref, rest_hbm, q_ref, acc_ref, seam_ref, gain_ref, wk_ref, wv_ref, wo_ref, *refs,
):
    out_ref, kbd, vbd, vsm, ksm, mixed, packed, rest_ref, wkt_ref, kt_ref, vo_ref, at_row, done = refs[-13:]
    blocks = refs[:-13]
    rows = x_ref.shape[0]
    count = rows // WIN
    pairs = count // 2
    near = 2 * SEAM
    step = pl.program_id(0)
    first_window = step * count

    def lanes_of(k):
        return jnp.where(lax.broadcasted_iota(jnp.int32, (1, 128), 1) // DIM == k, 1.0, 0.0).astype(BF)

    position = lax.broadcasted_iota(jnp.int32, (WIN, 1), 0)

    @pl.when(step == 0)
    def _():
        at_row[0] = 0
        wkt_ref[...] = wk_ref[...].astype(F32).T.astype(BF)
        packed[0:LIMIT, :] = main_ref[...].astype(F32)

        def add(w, total):
            return total + sent(offset_ref[w])

        @pl.when(lax.fori_loop(0, pl.num_programs(0) * count, add, 0) > LIMIT)
        def _():
            copy = pltpu.make_async_copy(rest_hbm, rest_ref, done)
            copy.start()
            copy.wait()
            packed[LIMIT:, :] = rest_ref[...].astype(F32)

        kbd[...] = jnp.zeros(kbd.shape, BF)
        vsm[...] = jnp.zeros(vsm.shape, BF)
        for half in range(2):
            for k in range(HALF):
                for w in range(count):
                    vbd[w, half, k * WIN:k * WIN + WIN, 128:256] = jnp.broadcast_to(lanes_of(k), (WIN, 128))
                h = half * HALF + k
                for p in range(pairs):
                    vsm[p, h * near:h * near + near, half * C + 128:half * C + C] = jnp.broadcast_to(
                        lanes_of(k), (near, 128)
                    )

    block = (lax.broadcasted_iota(jnp.int32, (64, 128), 0) // DIM) == (
        lax.broadcasted_iota(jnp.int32, (64, 128), 1) // WIN
    )
    first_lanes = lax.broadcasted_iota(jnp.int32, (64, 128), 1) < WIN
    own = (lax.broadcasted_iota(jnp.int32, (128, 128), 1) % near) // SEAM == (
        lax.broadcasted_iota(jnp.int32, (128, 128), 0) // WIN
    )
    some = count // PIECES
    some_pairs = some // 2

    def build(piece):
        w0 = piece * some
        p0 = piece * some_pairs
        chosen = []
        start = at_row[0]
        for w in range(w0, w0 + some):
            offset = offset_ref[first_window + w]
            other = packed[pl.ds(pl.multiple_of(start, 8), WIN), :]
            chosen.append(jnp.where(position >= offset, x_ref[w * WIN:w * WIN + WIN, :].astype(F32), other))
            start = start + sent(offset)
        at_row[0] = start
        normed = norm_rows(jnp.concatenate(chosen, axis=0), gain_ref[...])
        keys = dot_nt(wkt_ref[...], normed)
        values = dot(normed, wv_ref[...]).astype(BF)
        for half in range(2):
            for b in range(2):
                lo = half * 128 + b * 64
                for p in range(some_pairs):
                    pair = keys[lo:lo + 64, p * 128:p * 128 + 128]
                    turn = pltpu.roll(pair, WIN, 1)
                    to = (half, slice(b * 64, b * 64 + 64), slice(b * 128, b * 128 + 128))
                    w = w0 + 2 * p
                    kbd[(w,) + to] = jnp.where(block, jnp.where(first_lanes, pair, turn), 0.0).astype(BF)
                    kbd[(w + 1,) + to] = jnp.where(block, jnp.where(first_lanes, turn, pair), 0.0).astype(BF)
            for k in range(HALF):
                for w in range(some):
                    vbd[w0 + w, half, k * WIN:k * WIN + WIN, 0:128] = (
                        values[w * WIN:w * WIN + WIN, half * 128:half * 128 + 128] * lanes_of(k)
                    )

        wide = some_pairs * 128
        rows_s = some * SEAM
        seam_in = seam_ref[piece * rows_s:piece * rows_s + rows_s, :]
        seam_k = dot_nt(wkt_ref[...], seam_in).astype(BF)
        column = lax.broadcasted_iota(jnp.int32, (rows_s, wide), 1)
        spread = jnp.where(
            lax.broadcasted_iota(jnp.int32, (rows_s, wide), 0) == column // 128 * near + column % near, 1.0, 0.0
        ).astype(BF)
        of_head = (lax.broadcasted_iota(jnp.int32, (C, wide), 1) % 128) // near == (
            lax.broadcasted_iota(jnp.int32, (C, wide), 0) // DIM
        )
        seam_kt = jnp.where(of_head, dot(seam_k, spread), 0.0).astype(BF)
        seam_v = dot(seam_in, wv_ref[...]).astype(BF)
        for p in range(some_pairs):
            ksm[p0 + p] = seam_kt[:, p * 128:p * 128 + 128]
            for h in range(HEADS):
                half, k = h // HALF, h % HALF
                vsm[p0 + p, h * near:h * near + near, half * C:half * C + 128] = (
                    seam_v[p * near:p * near + near, half * 128:half * 128 + 128] * lanes_of(k)
                )

    def window_scores(w, half):
        at = pl.ds(pl.multiple_of(w * WIN, WIN), WIN)
        return dot(q_ref[at, half * 128:half * 128 + 128], kbd[w, half])

    def seam_scores(p):
        return dot(q_ref[pl.ds(pl.multiple_of(p * 128, 128), 128), :], ksm[p])

    def weigh(piece):
        pairs_here = range(piece * some_pairs, piece * some_pairs + some_pairs)
        windows_here = range(piece * some, piece * some + some)
        weights_s = [jnp.where(own, exp2(seam_scores(p)), 0.0).astype(BF) for p in pairs_here]
        weights_w = [[exp2(window_scores(w, half)).astype(BF) for half in range(2)] for w in windows_here]
        return weights_s, weights_w

    def add_up(piece, weights):
        weights_s, weights_w = weights
        check = jnp.zeros((8, 128), F32)
        for p in range(some_pairs):
            lo = (piece * some_pairs + p) * 128
            base = acc_ref[lo:lo + 128, :] + dot(weights_s[p], vsm[piece * some_pairs + p])
            for half in range(2):
                total = base[:, half * C:half * C + C] + jnp.concatenate(
                    [dot(weights_w[2 * p + w][half], vbd[piece * some + 2 * p + w, half]) for w in range(2)], axis=0
                )
                den = total[:, 128:256]
                inverse = 1.0 / den
                check = check + jnp.sum((den + inverse).reshape(16, 8, 128), axis=0)
                mixed[lo:lo + 128, half * 128:half * 128 + 128] = (total[:, 0:128] * inverse).astype(BF)
        return check

    def finish(piece):
        at = slice(piece * some * WIN, piece * some * WIN + some * WIN)
        out_ref[at, :] = (x_ref[at, :].astype(F32) + dot(mixed[at, :], wo_ref[...])).astype(BF)

    build(0)
    check = jnp.zeros((8, 128), F32)
    for piece in range(PIECES):
        weights = weigh(piece)
        if piece + 1 < PIECES:
            build(piece + 1)
        check = check + add_up(piece, weights)
        if piece > 0:
            finish(piece - 1)
    finish(PIECES - 1)
    fine = jnp.sum(check) <= HIGH

    @pl.when(jnp.logical_not(fine))
    def _():
        lay_out_group(blocks, wk_ref, wv_ref, kt_ref, vo_ref)
        keys_g = kt_ref.shape[2]
        head_s = lax.broadcasted_iota(jnp.int32, (128, 128), 1) // near
        head_w = lax.broadcasted_iota(jnp.int32, (128, C), 1) // WIN

        def exact(p, carry):
            at = pl.ds(pl.multiple_of(p * 128, 128), 128)
            scores_s = jnp.where(own, seam_scores(p), NEG)
            tops_s = jnp.zeros((128, 128), F32)
            totals = []
            for half in range(2):
                q = q_ref[at, half * 128:half * 128 + 128]
                scores_w = jnp.concatenate([window_scores(2 * p + w, half) for w in range(2)], axis=0)
                tops_w = jnp.zeros((128, C), F32)
                total = jnp.zeros((128, C), F32)
                for k in range(HALF):
                    h = half * HALF + k
                    scores_g = dot(q, kt_ref[h])
                    top = jnp.max(scores_g, axis=1, keepdims=True)
                    top = jnp.maximum(top, jnp.max(jnp.where(head_s == h, scores_s, NEG), axis=1, keepdims=True))
                    top = jnp.maximum(top, jnp.max(jnp.where(head_w == k, scores_w, NEG), axis=1, keepdims=True))
                    tops_s = jnp.where(head_s == h, top, tops_s)
                    tops_w = jnp.where(head_w == k, top, tops_w)
                    total = total + dot(
                        exp2(scores_g - top).astype(BF), vo_ref[half, k * keys_g:k * keys_g + keys_g]
                    )
                weights = exp2(scores_w - tops_w).astype(BF)
                totals.append(total + jnp.concatenate(
                    [dot(weights[w * WIN:w * WIN + WIN], vbd[2 * p + w, half]) for w in range(2)], axis=0
                ))
            weights = jnp.where(own, exp2(jnp.where(own, scores_s - tops_s, NEG)), 0.0).astype(BF)
            total = jnp.concatenate(totals, axis=1) + dot(weights, vsm[p])
            again = jnp.concatenate(
                [total[:, half * C:half * C + 128] / total[:, half * C + 128:half * C + C] for half in range(2)], axis=1
            ).astype(BF)
            out_ref[at, :] = (x_ref[at, :].astype(F32) + dot(again, wo_ref[...])).astype(BF)
            return carry

        lax.fori_loop(0, pairs, exact, 0)


def window(offsets, x, main, rest, q, acc, seam_rows, gain, w_qkv, wo, blocks, rows=2048):
    pixels = x.shape[0]
    count = rows // WIN
    row = lambda i, s: (i, 0)
    fixed = lambda i, s: (0, 0)
    return pl.pallas_call(
        window_body,
        grid_spec=pltpu.PrefetchScalarGridSpec(
            num_scalar_prefetch=1,
            grid=(pixels // rows,),
            in_specs=[
                pl.BlockSpec((rows, C), row),
                pl.BlockSpec(main.shape, fixed),
                pl.BlockSpec(memory_space=pl.ANY),
                pl.BlockSpec((rows, C), row),
                pl.BlockSpec((rows, 2 * C), row),
                pl.BlockSpec((count * SEAM, C), row),
                pl.BlockSpec((1, C), fixed),
                pl.BlockSpec((C, C), lambda i, s: (0, 1)),
                pl.BlockSpec((C, C), lambda i, s: (0, 2)),
                pl.BlockSpec((C, C), fixed),
            ]
            + [pl.BlockSpec(b.shape, fixed) for b in blocks],
            out_specs=pl.BlockSpec((rows, C), row),
            scratch_shapes=[
                pltpu.VMEM((count, 2, 128, C), BF),
                pltpu.VMEM((count, 2, HALF * WIN, C), BF),
                pltpu.VMEM((count // 2, 128, 2 * C), BF),
                pltpu.VMEM((count // 2, C, 128), BF),
                pltpu.VMEM((rows, C), BF),
                pltpu.VMEM((pixels, C), F32),
                pltpu.VMEM(rest.shape, BF),
                pltpu.VMEM((C, C), BF),
                *group_scratch(blocks),
                pltpu.SMEM((1,), jnp.int32),
                pltpu.SemaphoreType.DMA,
            ],
        ),
        out_shape=jax.ShapeDtypeStruct((pixels, C), BF),
        compiler_params=params(60),
        cost_estimate=pl.CostEstimate(
            flops=40 * pixels * C * C, bytes_accessed=20 * pixels * C, transcendentals=0
        ),
        name="window_attention",
    )(offsets, x, main, rest, q, acc, seam_rows, gain, w_qkv, w_qkv, wo, *blocks)


def rotation(dx, dz, dy):
    pairs = []
    for f in range(32):
        x, z, y = f // 8, f // 4 % 2, f % 4
        pairs.append((f, (x + dx) % 4 * 8 + (z + dz) % 2 * 4 + (y + dy) % 4))
    return pairs


def partner(x):
    return lax.ppermute(x, "face", [(i, i ^ 1) for i in range(32)])


def turned(block, steps):
    return [block] + [lax.ppermute(block, "face", rotation(*s)) for s in steps]


def place_in_pool(index, windows):
    face, local = index // windows, index % windows
    me = lax.axis_index("face")
    dx = (me // 8 - face // 8) % 4
    dz = (me // 4 - face // 4) % 2
    dy = (me - face) % 4
    return ((dx * 2 + dz) * 4 + dy) * windows + local


def by_sub(x, k):
    return lax.ppermute(x, "sub", [(i, i ^ k) for i in range(4)])


def local(pixel_state, norm1_gain, w_qkv, w_out, shift_offsets, seam_table):
    pixels = pixel_state.shape[0]
    gain = norm1_gain.reshape(1, C)
    asked = partner(shift_offsets)
    pooled, asked = lax.optimization_barrier((pool_rows(pixel_state, gain), asked))
    groups = [pooled] + [by_sub(pooled, k) for k in (1, 2, 3)]
    columns = turned(pooled, [(0, 0, 1), (0, 0, 2), (0, 0, 3)])
    main, rest, more = pack(asked, shift_offsets, pixel_state)
    main = partner(main)
    planes = turned(join(*columns), [(0, 1, 0)])
    cube = join(*planes)
    pools = turned(cube, [(1, 0, 0), (2, 0, 0), (3, 0, 0)])
    split = pixels // 4
    sums = coarse(0, split, pixel_state, gain, w_qkv, groups, gain, rows=512)
    q, acc = coarse(split, pixels - split, pixel_state, gain, w_qkv, groups, cube, sums)
    index = place_in_pool(seam_table, pooled.shape[0]).reshape(-1, 1)
    seam_rows = seam(index, pools)
    _, rest = lax.while_loop(lambda c: c[0] > 0, lambda c: (c[0] - 1, partner(c[1])), (more[0], rest))
    return window(shift_offsets, pixel_state, main, rest, q, acc, seam_rows, gain, w_qkv, w_out, groups)


def solution(mesh):
    return jax.shard_map(
        local,
        mesh=mesh,
        in_specs=(
            P(("face", "sub"), None),
            P(),
            P(),
            P(),
            P(("face", "sub")),
            P(("face", "sub"), None),
        ),
        out_specs=P(("face", "sub"), None),
        check_vma=False,
    )
```

```python
import functools
import math

import jax
import jax.numpy as jnp
from jax import lax
from jax.experimental import pallas as pl
from jax.experimental.pallas import tpu as pltpu
from jax.sharding import PartitionSpec as P

HEADS = 8
HALF = HEADS // 2
DIM = 32
C = 256
WIN = 64
SEAM = 8
EPS = 1e-05
SCALE = math.log2(math.e) / math.sqrt(DIM)
BF = jnp.bfloat16
F32 = jnp.float32
HIGH = 2.0 ** 100
NEG = -1e30
MB = 1024 * 1024
LIMIT = 5360
PIECES = 2


def params(limit):
    return pltpu.CompilerParams(vmem_limit_bytes=limit * MB)


def exp2(x):
    return jnp.exp2(x)


def dot(a, b):
    return jnp.dot(a, b, preferred_element_type=F32)


def dot_nt(a, b):
    return lax.dot_general(a, b, (((1,), (1,)), ((), ())), preferred_element_type=F32)


def sent(offset):
    return (offset + 7) // 8 * 8


def norm_rows(x, gain):
    centre = jnp.mean(x, axis=-1, keepdims=True)
    x = x - centre
    spread = jnp.mean(x * x, axis=-1, keepdims=True)
    return (x * lax.rsqrt(spread + EPS) * gain).astype(BF)


def pool_body(x_ref, gain_ref, pooled_ref):
    rows = x_ref.shape[0]
    normed = norm_rows(x_ref[...].astype(F32), gain_ref[...])
    count = rows // WIN
    row = lax.broadcasted_iota(jnp.int32, (count, rows), 1) // WIN
    pick = jnp.where(row == lax.broadcasted_iota(jnp.int32, (count, rows), 0), 1.0, 0.0).astype(BF)
    pooled_ref[...] = (dot(pick, normed) * (1.0 / math.sqrt(WIN))).astype(BF)


def pool_rows(x, gain, rows=2048):
    pixels = x.shape[0]
    return pl.pallas_call(
        pool_body,
        grid=(pixels // rows,),
        in_specs=[
            pl.BlockSpec((rows, C), lambda i: (i, 0)),
            pl.BlockSpec((1, C), lambda i: (0, 0)),
        ],
        out_specs=pl.BlockSpec((rows // WIN, C), lambda i: (i, 0)),
        out_shape=jax.ShapeDtypeStruct((pixels // WIN, C), BF),
        compiler_params=params(60),
        cost_estimate=pl.CostEstimate(flops=2 * pixels * C * C, bytes_accessed=4 * pixels * C, transcendentals=0),
        name="norm_pool",
    )(x, gain)


def pack_body(offset_ref, mine_ref, x_ref, main_ref, rest_hbm, more_ref, packed, rest_ref, at_row, done):
    step = pl.program_id(0)
    count = x_ref.shape[0] // WIN
    @pl.when(step == 0)
    def _():
        at_row[0] = 0

    start = at_row[0]
    for w in range(count):
        packed[pl.ds(pl.multiple_of(start, 8), WIN), :] = x_ref[w * WIN:w * WIN + WIN, :].astype(F32)
        start = start + sent(offset_ref[step * count + w])
    at_row[0] = start

    @pl.when(step == pl.num_programs(0) - 1)
    def _():
        main_ref[...] = packed[0:LIMIT, :].astype(BF)
        mine = lax.fori_loop(0, mine_ref.shape[0], lambda w, total: total + sent(mine_ref[w]), 0)
        more_ref[0] = (jnp.maximum(start, mine) > LIMIT).astype(jnp.int32)

        @pl.when(start > LIMIT)
        def _():
            rest_ref[...] = packed[LIMIT:, :].astype(BF)
            copy = pltpu.make_async_copy(rest_ref, rest_hbm, done)
            copy.start()
            copy.wait()


def pack(offsets, mine, x, rows=4096):
    pixels = x.shape[0]
    whole = lambda i, s, t: (0, 0)
    return pl.pallas_call(
        pack_body,
        grid_spec=pltpu.PrefetchScalarGridSpec(
            num_scalar_prefetch=2,
            grid=(pixels // rows,),
            in_specs=[pl.BlockSpec((rows, C), lambda i, s, t: (i, 0))],
            out_specs=[
                pl.BlockSpec((LIMIT, C), whole),
                pl.BlockSpec(memory_space=pl.ANY),
                pl.BlockSpec(memory_space=pltpu.SMEM),
            ],
            scratch_shapes=[
                pltpu.VMEM((pixels, C), F32),
                pltpu.VMEM((pixels - LIMIT, C), BF),
                pltpu.SMEM((1,), jnp.int32),
                pltpu.SemaphoreType.DMA,
            ],
        ),
        out_shape=[
            jax.ShapeDtypeStruct((LIMIT, C), BF),
            jax.ShapeDtypeStruct((pixels - LIMIT, C), BF),
            jax.ShapeDtypeStruct((1,), jnp.int32),
        ],
        compiler_params=params(60),
        cost_estimate=pl.CostEstimate(flops=0, bytes_accessed=10 * pixels * C, transcendentals=0),
        name="pack_rows",
    )(offsets, mine, x)


def join_body(*refs):
    lo = 0
    for ref in refs[:-1]:
        refs[-1][lo:lo + ref.shape[0]] = ref[...]
        lo += ref.shape[0]


def join(*blocks):
    rows = sum(b.shape[0] for b in blocks)
    return pl.pallas_call(
        join_body, out_shape=jax.ShapeDtypeStruct((rows, C), BF), compiler_params=params(32), name="join_blocks"
    )(*blocks)


def lay_out_group(blocks, wk_ref, wv_ref, kt_ref, vo_ref):
    g = jnp.concatenate([ref[...] for ref in blocks], axis=0)
    count = g.shape[0]
    kt = lax.dot_general(wk_ref[...], g, (((0,), (1,)), ((), ())), preferred_element_type=F32)
    v = dot(g, wv_ref[...])
    feat = lax.broadcasted_iota(jnp.int32, (128, count), 0) // DIM
    lane = lax.broadcasted_iota(jnp.int32, (count, 128), 1) // DIM
    for h in range(HEADS):
        half, k = h // HALF, h % HALF
        kt_ref[h] = jnp.where(feat == k, kt[half * 128:half * 128 + 128], 0.0).astype(BF)
        vo_ref[half, k * count:k * count + count, 0:128] = jnp.where(
            lane == k, v[:, half * 128:half * 128 + 128], 0.0
        ).astype(BF)
        vo_ref[half, k * count:k * count + count, 128:256] = jnp.where(lane == k, 1.0, 0.0).astype(BF)


def group_scratch(blocks):
    count = sum(b.shape[0] for b in blocks)
    return [pltpu.VMEM((HEADS, 128, count), BF), pltpu.VMEM((2, HALF * count, C), BF)]


def coarse_body(blocks, x_ref, next_ref, gain_ref, wq_ref, wk_ref, wv_ref, *refs):
    q_ref, acc_ref, held, kt_ref, vo_ref = refs[-5:]
    step = pl.program_id(0)

    def queries(ref):
        return (dot(norm_rows(ref[...].astype(F32), gain_ref[...]), wq_ref[...]) * SCALE).astype(BF)

    @pl.when(step == 0)
    def _():
        lay_out_group(refs[:blocks], wk_ref, wv_ref, kt_ref, vo_ref)
        held[...] = queries(x_ref)

    q = held[...]
    q_ref[...] = q
    weights = []
    for half in range(2):
        heads = range(half * HALF, half * HALF + HALF)
        mine = q[:, half * 128:half * 128 + 128]
        weights.append(jnp.concatenate([exp2(dot(mine, kt_ref[h])).astype(BF) for h in heads], axis=1))
    acc_ref[:, 0:C] = dot(weights[0], vo_ref[0])
    acc_ref[:, C:2 * C] = dot(weights[1], vo_ref[1])
    held[...] = queries(next_ref)


def coarse(first, run, x, gain, w_qkv, blocks, after, given=(), rows=1024):
    pixels = x.shape[0]
    steps = run // rows
    base = first // rows
    count = sum(b.shape[0] for b in blocks)
    fixed = 6 + len(blocks) + 1
    return pl.pallas_call(
        functools.partial(coarse_body, len(blocks)),
        grid=(steps,),
        in_specs=[
            pl.BlockSpec((rows, C), lambda i: (base, 0)),
            pl.BlockSpec((rows, C), lambda i: (base + jnp.minimum(i + 1, steps - 1), 0)),
            pl.BlockSpec((1, C), lambda i: (0, 0)),
            pl.BlockSpec((C, C), lambda i: (0, 0)),
            pl.BlockSpec((C, C), lambda i: (0, 1)),
            pl.BlockSpec((C, C), lambda i: (0, 2)),
        ]
        + [pl.BlockSpec(b.shape, lambda i: (0, 0)) for b in blocks]
        + [pl.BlockSpec(memory_space=pl.ANY)] * (1 + len(given)),
        out_specs=[
            pl.BlockSpec((rows, C), lambda i: (base + i, 0)),
            pl.BlockSpec((rows, 2 * C), lambda i: (base + i, 0)),
        ],
        out_shape=[
            jax.ShapeDtypeStruct((pixels, C), BF),
            jax.ShapeDtypeStruct((pixels, 2 * C), F32),
        ],
        scratch_shapes=[pltpu.VMEM((rows, C), BF)] + group_scratch(blocks),
        input_output_aliases={fixed: 0, fixed + 1: 1} if given else {},
        compiler_params=params(60),
        cost_estimate=pl.CostEstimate(
            flops=4 * run * HEADS * count * C, bytes_accessed=10 * run * C, transcendentals=run * HEADS * count
        ),
        name="group_attention",
    )(x, x, gain, w_qkv, w_qkv, w_qkv, *blocks, after, *given)


def seam_body(index_ref, *refs):
    out_ref = refs[-1]
    rows = index_ref.shape[0]
    total = jnp.zeros((rows, C), F32)
    lo = 0
    for ref in refs[:-1]:
        step = ref.shape[0]
        at = lax.broadcasted_iota(jnp.int32, (rows, step), 1) + lo
        pick = jnp.where(at == index_ref[...], 1.0, 0.0).astype(BF)
        total = total + dot(pick, ref[...])
        lo += step
    out_ref[...] = total.astype(BF)


def seam(index, pools, rows=256):
    count = index.shape[0]
    return pl.pallas_call(
        seam_body,
        grid=(count // rows,),
        in_specs=[pl.BlockSpec((rows, 1), lambda i: (i, 0))]
        + [pl.BlockSpec(pool.shape, lambda i: (0, 0)) for pool in pools],
        out_specs=pl.BlockSpec((rows, C), lambda i: (i, 0)),
        out_shape=jax.ShapeDtypeStruct((count, C), BF),
        compiler_params=params(48),
        name="seam_rows",
    )(index, *pools)


def window_body(
    offset_ref, x_ref, main_ref, rest_hbm, q_ref, acc_ref, seam_ref, gain_ref, wk_ref, wv_ref, wo_ref, *refs,
):
    out_ref, kbd, vbd, vsm, ones_w, ones_s, ksm, mixed, packed, rest_ref, wkt_ref, kt_ref, vo_ref, at_row, done = refs[-15:]
    blocks = refs[:-15]
    rows = x_ref.shape[0]
    count = rows // WIN
    pairs = count // 2
    near = 2 * SEAM
    step = pl.program_id(0)
    first_window = step * count

    def lanes_of(k):
        return jnp.where(lax.broadcasted_iota(jnp.int32, (1, 128), 1) // DIM == k, 1.0, 0.0).astype(BF)

    position = lax.broadcasted_iota(jnp.int32, (WIN, 1), 0)

    @pl.when(step == 0)
    def _():
        at_row[0] = 0
        wkt_ref[...] = wk_ref[...].astype(F32).T.astype(BF)
        packed[0:LIMIT, :] = main_ref[...].astype(F32)

        def add(w, total):
            return total + sent(offset_ref[w])

        @pl.when(lax.fori_loop(0, pl.num_programs(0) * count, add, 0) > LIMIT)
        def _():
            copy = pltpu.make_async_copy(rest_hbm, rest_ref, done)
            copy.start()
            copy.wait()
            packed[LIMIT:, :] = rest_ref[...].astype(F32)

        for k in range(HALF):
            ones_w[k * WIN:k * WIN + WIN, :] = jnp.broadcast_to(lanes_of(k), (WIN, 128))
            ones_s[k * near:k * near + near, :] = jnp.broadcast_to(lanes_of(k), (near, 128))

    block = (lax.broadcasted_iota(jnp.int32, (64, 128), 0) // DIM) == (
        lax.broadcasted_iota(jnp.int32, (64, 128), 1) // WIN
    )
    first_lanes = lax.broadcasted_iota(jnp.int32, (64, 128), 1) < WIN
    own = (lax.broadcasted_iota(jnp.int32, (128, 128), 1) % near) // SEAM == (
        lax.broadcasted_iota(jnp.int32, (128, 128), 0) // WIN
    )
    some = count // PIECES
    some_pairs = some // 2

    def build(piece):
        w0 = piece * some
        p0 = piece * some_pairs
        chosen = []
        start = at_row[0]
        for w in range(w0, w0 + some):
            offset = offset_ref[first_window + w]
            other = packed[pl.ds(pl.multiple_of(start, 8), WIN), :]
            chosen.append(jnp.where(position >= offset, x_ref[w * WIN:w * WIN + WIN, :].astype(F32), other))
            start = start + sent(offset)
        at_row[0] = start
        normed = norm_rows(jnp.concatenate(chosen, axis=0), gain_ref[...])
        keys = dot_nt(wkt_ref[...], normed)
        values = dot(normed, wv_ref[...]).astype(BF)
        for half in range(2):
            for b in range(2):
                lo = half * 128 + b * 64
                for p in range(some_pairs):
                    pair = keys[lo:lo + 64, p * 128:p * 128 + 128]
                    turn = pltpu.roll(pair, WIN, 1)
                    to = (half, b)
                    w = w0 + 2 * p
                    kbd[(w,) + to] = jnp.where(block, jnp.where(first_lanes, pair, turn), 0.0).astype(BF)
                    kbd[(w + 1,) + to] = jnp.where(block, jnp.where(first_lanes, turn, pair), 0.0).astype(BF)
            for k in range(HALF):
                for w in range(some):
                    vbd[w0 + w, half, k * WIN:k * WIN + WIN, :] = (
                        values[w * WIN:w * WIN + WIN, half * 128:half * 128 + 128] * lanes_of(k)
                    )

        wide = some_pairs * 128
        rows_s = some * SEAM
        seam_in = seam_ref[piece * rows_s:piece * rows_s + rows_s, :]
        seam_k = dot_nt(wkt_ref[...], seam_in).astype(BF)
        column = lax.broadcasted_iota(jnp.int32, (rows_s, wide), 1)
        spread = jnp.where(
            lax.broadcasted_iota(jnp.int32, (rows_s, wide), 0) == column // 128 * near + column % near, 1.0, 0.0
        ).astype(BF)
        of_head = (lax.broadcasted_iota(jnp.int32, (C, wide), 1) % 128) // near == (
            lax.broadcasted_iota(jnp.int32, (C, wide), 0) // DIM
        )
        seam_kt = jnp.where(of_head, dot(seam_k, spread), 0.0).astype(BF)
        seam_v = dot(seam_in, wv_ref[...]).astype(BF)
        for p in range(some_pairs):
            ksm[p0 + p] = seam_kt[:, p * 128:p * 128 + 128]
            for h in range(HEADS):
                half, k = h // HALF, h % HALF
                vsm[p0 + p, half, k * near:k * near + near, :] = (
                    seam_v[p * near:p * near + near, half * 128:half * 128 + 128] * lanes_of(k)
                )

    gap = jnp.zeros((64, 128), BF)

    def window_keys(w, half):
        top = jnp.concatenate([kbd[w, half, 0], gap], axis=1)
        return jnp.concatenate([top, jnp.concatenate([gap, kbd[w, half, 1]], axis=1)], axis=0)

    def window_values(w, half):
        return jnp.concatenate([vbd[w, half], ones_w[...]], axis=1)

    def seam_values(p):
        top = jnp.concatenate([vsm[p, 0], ones_s[...], gap, gap], axis=1)
        return jnp.concatenate([top, jnp.concatenate([gap, gap, vsm[p, 1], ones_s[...]], axis=1)], axis=0)

    def window_scores(w, half):
        at = pl.ds(pl.multiple_of(w * WIN, WIN), WIN)
        return dot(q_ref[at, half * 128:half * 128 + 128], window_keys(w, half))

    def seam_scores(p):
        return dot(q_ref[pl.ds(pl.multiple_of(p * 128, 128), 128), :], ksm[p])

    def weigh(piece):
        pairs_here = range(piece * some_pairs, piece * some_pairs + some_pairs)
        windows_here = range(piece * some, piece * some + some)
        weights_s = [jnp.where(own, exp2(seam_scores(p)), 0.0).astype(BF) for p in pairs_here]
        weights_w = [[exp2(window_scores(w, half)).astype(BF) for half in range(2)] for w in windows_here]
        return weights_s, weights_w

    def add_up(piece, weights):
        weights_s, weights_w = weights
        check = jnp.zeros((8, 128), F32)
        for p in range(some_pairs):
            lo = (piece * some_pairs + p) * 128
            base = acc_ref[lo:lo + 128, :] + dot(weights_s[p], seam_values(piece * some_pairs + p))
            for half in range(2):
                total = base[:, half * C:half * C + C] + jnp.concatenate(
                    [dot(weights_w[2 * p + w][half], window_values(piece * some + 2 * p + w, half)) for w in range(2)], axis=0
                )
                den = total[:, 128:256]
                inverse = 1.0 / den
                check = check + jnp.sum((den + inverse).reshape(16, 8, 128), axis=0)
                mixed[lo:lo + 128, half * 128:half * 128 + 128] = (total[:, 0:128] * inverse).astype(BF)
        return check

    def finish(piece):
        at = slice(piece * some * WIN, piece * some * WIN + some * WIN)
        out_ref[at, :] = (x_ref[at, :].astype(F32) + dot(mixed[at, :], wo_ref[...])).astype(BF)

    build(0)
    check = jnp.zeros((8, 128), F32)
    for piece in range(PIECES):
        weights = weigh(piece)
        if piece + 1 < PIECES:
            build(piece + 1)
        check = check + add_up(piece, weights)
        if piece > 0:
            finish(piece - 1)
    finish(PIECES - 1)
    fine = jnp.sum(check) <= HIGH

    @pl.when(jnp.logical_not(fine))
    def _():
        lay_out_group(blocks, wk_ref, wv_ref, kt_ref, vo_ref)
        keys_g = kt_ref.shape[2]
        head_s = lax.broadcasted_iota(jnp.int32, (128, 128), 1) // near
        head_w = lax.broadcasted_iota(jnp.int32, (128, C), 1) // WIN

        def exact(p, carry):
            at = pl.ds(pl.multiple_of(p * 128, 128), 128)
            scores_s = jnp.where(own, seam_scores(p), NEG)
            tops_s = jnp.zeros((128, 128), F32)
            totals = []
            for half in range(2):
                q = q_ref[at, half * 128:half * 128 + 128]
                scores_w = jnp.concatenate([window_scores(2 * p + w, half) for w in range(2)], axis=0)
                tops_w = jnp.zeros((128, C), F32)
                total = jnp.zeros((128, C), F32)
                for k in range(HALF):
                    h = half * HALF + k
                    scores_g = dot(q, kt_ref[h])
                    top = jnp.max(scores_g, axis=1, keepdims=True)
                    top = jnp.maximum(top, jnp.max(jnp.where(head_s == h, scores_s, NEG), axis=1, keepdims=True))
                    top = jnp.maximum(top, jnp.max(jnp.where(head_w == k, scores_w, NEG), axis=1, keepdims=True))
                    tops_s = jnp.where(head_s == h, top, tops_s)
                    tops_w = jnp.where(head_w == k, top, tops_w)
                    total = total + dot(
                        exp2(scores_g - top).astype(BF), vo_ref[half, k * keys_g:k * keys_g + keys_g]
                    )
                weights = exp2(scores_w - tops_w).astype(BF)
                totals.append(total + jnp.concatenate(
                    [dot(weights[w * WIN:w * WIN + WIN], window_values(2 * p + w, half)) for w in range(2)], axis=0
                ))
            weights = jnp.where(own, exp2(jnp.where(own, scores_s - tops_s, NEG)), 0.0).astype(BF)
            total = jnp.concatenate(totals, axis=1) + dot(weights, seam_values(p))
            again = jnp.concatenate(
                [total[:, half * C:half * C + 128] / total[:, half * C + 128:half * C + C] for half in range(2)], axis=1
            ).astype(BF)
            out_ref[at, :] = (x_ref[at, :].astype(F32) + dot(again, wo_ref[...])).astype(BF)
            return carry

        lax.fori_loop(0, pairs, exact, 0)


def window(offsets, x, main, rest, q, acc, seam_rows, gain, w_qkv, wo, blocks, rows=2048):
    pixels = x.shape[0]
    count = rows // WIN
    row = lambda i, s: (i, 0)
    fixed = lambda i, s: (0, 0)
    return pl.pallas_call(
        window_body,
        grid_spec=pltpu.PrefetchScalarGridSpec(
            num_scalar_prefetch=1,
            grid=(pixels // rows,),
            in_specs=[
                pl.BlockSpec((rows, C), row),
                pl.BlockSpec(main.shape, fixed),
                pl.BlockSpec(memory_space=pl.ANY),
                pl.BlockSpec((rows, C), row),
                pl.BlockSpec((rows, 2 * C), row),
                pl.BlockSpec((count * SEAM, C), row),
                pl.BlockSpec((1, C), fixed),
                pl.BlockSpec((C, C), lambda i, s: (0, 1)),
                pl.BlockSpec((C, C), lambda i, s: (0, 2)),
                pl.BlockSpec((C, C), fixed),
            ]
            + [pl.BlockSpec(b.shape, fixed) for b in blocks],
            out_specs=pl.BlockSpec((rows, C), row),
            scratch_shapes=[
                pltpu.VMEM((count, 2, 2, 64, 128), BF),
                pltpu.VMEM((count, 2, HALF * WIN, 128), BF),
                pltpu.VMEM((count // 2, 2, 64, 128), BF),
                pltpu.VMEM((HALF * WIN, 128), BF),
                pltpu.VMEM((64, 128), BF),
                pltpu.VMEM((count // 2, C, 128), BF),
                pltpu.VMEM((rows, C), BF),
                pltpu.VMEM((pixels, C), F32),
                pltpu.VMEM(rest.shape, BF),
                pltpu.VMEM((C, C), BF),
                *group_scratch(blocks),
                pltpu.SMEM((1,), jnp.int32),
                pltpu.SemaphoreType.DMA,
            ],
        ),
        out_shape=jax.ShapeDtypeStruct((pixels, C), BF),
        compiler_params=params(60),
        cost_estimate=pl.CostEstimate(
            flops=40 * pixels * C * C, bytes_accessed=20 * pixels * C, transcendentals=0
        ),
        name="window_attention",
    )(offsets, x, main, rest, q, acc, seam_rows, gain, w_qkv, w_qkv, wo, *blocks)


def rotation(dx, dz, dy):
    pairs = []
    for f in range(32):
        x, z, y = f // 8, f // 4 % 2, f % 4
        pairs.append((f, (x + dx) % 4 * 8 + (z + dz) % 2 * 4 + (y + dy) % 4))
    return pairs


def partner(x):
    return lax.ppermute(x, "face", [(i, i ^ 1) for i in range(32)])


def turned(block, steps):
    return [block] + [lax.ppermute(block, "face", rotation(*s)) for s in steps]


def place_in_pool(index, windows):
    face, local = index // windows, index % windows
    me = lax.axis_index("face")
    dx = (me // 8 - face // 8) % 4
    dz = (me // 4 - face // 4) % 2
    dy = (me - face) % 4
    return ((dx * 2 + dz) * 4 + dy) * windows + local


def by_sub(x, k):
    return lax.ppermute(x, "sub", [(i, i ^ k) for i in range(4)])


def local(pixel_state, norm1_gain, w_qkv, w_out, shift_offsets, seam_table):
    pixels = pixel_state.shape[0]
    gain = norm1_gain.reshape(1, C)
    asked = partner(shift_offsets)
    pooled, asked = lax.optimization_barrier((pool_rows(pixel_state, gain), asked))
    groups = [pooled] + [by_sub(pooled, k) for k in (1, 2, 3)]
    columns = turned(pooled, [(0, 0, 1), (0, 0, 2), (0, 0, 3)])
    main, rest, more = pack(asked, shift_offsets, pixel_state)
    main = partner(main)
    planes = turned(join(*columns), [(0, 1, 0)])
    cube = join(*planes)
    pools = turned(cube, [(1, 0, 0), (2, 0, 0), (3, 0, 0)])
    split = pixels // 4
    sums = coarse(0, split, pixel_state, gain, w_qkv, groups, gain, rows=512)
    q, acc = coarse(split, pixels - split, pixel_state, gain, w_qkv, groups, cube, sums)
    index = place_in_pool(seam_table, pooled.shape[0]).reshape(-1, 1)
    seam_rows = seam(index, pools)
    _, rest = lax.while_loop(lambda c: c[0] > 0, lambda c: (c[0] - 1, partner(c[1])), (more[0], rest))
    return window(shift_offsets, pixel_state, main, rest, q, acc, seam_rows, gain, w_qkv, w_out, groups)


def solution(mesh):
    return jax.shard_map(
        local,
        mesh=mesh,
        in_specs=(
            P(("face", "sub"), None),
            P(),
            P(),
            P(),
            P(("face", "sub")),
            P(("face", "sub"), None),
        ),
        out_specs=P(("face", "sub"), None),
        check_vma=False,
    )
```
